32 devices in a mesh: space: 8 (over z, x), tm: 4 (over y, core).
Axes of the slice: x: 2, y: 2, z: 4, core: 2. Of those that a mesh axis runs over, the one named last changes fastest.
Arguments:
- eigvecs: float32 [4, 2, 3, 64, 8, 144], P('tm', None, None, None, 'space'), may hold values from -6 to 6
- gauge_links: float32 [3, 4, 2, 3, 3, 8, 144], P(None, 'tm', None, None, None, 'space'), may hold values from -4 to 4
- perambulators: bfloat16 [4, 4, 2, 4, 4, 64, 64], P('tm'), may hold values from -0.375 to 0.375
- momenta: int32 [32, 3], replicated, may hold values from -2 to 2, as said below
Outputs:
- smeared: bfloat16 [4, 2, 3, 64, 8, 144], P('tm', None, None, None, 'space')
- elementals: bfloat16 [32, 4, 2, 64, 64], P(None, 'tm')
- correlator: float32 [2, 32, 4, 4], P(None, None, 'tm')
The draws below stay inside these ranges and needn't reach their ends.
Inputs may be any that keep to these rules, and one draw needn't show every extreme that they name: `momenta`: every row is a nonzero vector of integers.
All inputs are finite; a program needn't handle non-finite values.
Results may differ from the reference program's by a relative error of at most 0.0053.
Values may be sent and summed in bfloat16 or wider, within the bound.
A program may use at most 128 MiB of HBM per device.

```python
import math
import jax
import jax.numpy as jnp
from jax import lax

NEV = 64
NP = 32
SPIN = 4
LX = 24
YB = 4
NT = 4
NZ = 2
ROWS = 6


def draw_momenta(key, part):
    sampled = jax.random.randint(key, (NP, 3), -2, 3, dtype=jnp.int32)
    zero_row = jnp.all(sampled == 0, axis=1)
    first_col = jnp.where(zero_row, 1, sampled[:, 0])
    sampled = jnp.concatenate([first_col[:, None], sampled[:, 1:]], axis=1)
    forced = jnp.array([[2, -2, 1]], dtype=jnp.int32)
    row_ids = jnp.arange(NP, dtype=jnp.int32)[:, None]
    return jnp.where(row_ids == 0, forced, sampled).astype(jnp.int32)


def block_scale(key, dims, split, smallest, top_value):
    factor_of = 1.0
    for position, shards_of in split:
        steps = jax.random.uniform(jax.random.fold_in(jax.random.fold_in(key, 6), position), (shards_of,), jnp.float32, smallest / len(split), top_value / len(split))
        factor_of = factor_of * jnp.repeat(jnp.exp(steps), dims[position] // shards_of).reshape((-1,) + (1,) * (len(dims) - 1 - position))
    return factor_of


def centred(own_key, extent, spread, limit, pieces=(), kind=jnp.bfloat16):
    factor_of = block_scale(own_key, extent, pieces, -0.22, 0.18) if pieces else 1.0
    values = jax.random.normal(own_key, extent, jnp.float32) * spread * factor_of
    return jnp.minimum(jnp.maximum(values, -limit), limit).astype(kind)


def setup_inputs(seed: int = 0) -> dict:
    key_of = jax.random.split(jax.random.key(seed), 5)
    eigvecs = centred(key_of[0], (NT, 2, 3, NEV, NZ * YB, ROWS * LX), 1.0, 6.0, ((0, 4), (4, 8)), jnp.float32)
    gauge_links = centred(key_of[1], (3, NT, 2, 3, 3, NZ * YB, ROWS * LX), 0.577, 4.0, ((1, 4), (5, 8)), jnp.float32)
    perambulators = centred(key_of[2], (NT, NT, 2, SPIN, SPIN, NEV, NEV), (NEV * SPIN) ** -0.5, 0.375, ((0, 4),))
    momenta = draw_momenta(jax.random.fold_in(key_of[4], 71), 0)
    return {"eigvecs": eigvecs, "gauge_links": gauge_links, "perambulators": perambulators, "momenta": momenta}


KAPPA = 0.25
op_group = 2

def move(lattice, direction, stride):
    layout = lattice.shape
    planes = lattice.reshape(layout[:-1] + (layout[-1] // LX, LX))
    if direction == 0:
        planes = jnp.roll(planes, -stride, axis=-1)
    elif direction == 1:
        planes = jnp.roll(planes, -stride, axis=-2)
    else:
        planes = jnp.roll(planes, -stride, axis=-3)
    return planes.reshape(layout)

def transport(one_link, vector, adjoint):
    link_re = one_link[..., 0, :, :, :, :]
    link_im = one_link[..., 1, :, :, :, :]
    vec_re = vector[..., 0, :, :, :, :]
    vec_im = vector[..., 1, :, :, :, :]
    out_re = 0.0
    out_im = 0.0
    for colour in range(3):
        if adjoint:
            factor_re = link_re[..., colour, :, None, :, :]
            factor_im = -link_im[..., colour, :, None, :, :]
        else:
            factor_re = link_re[..., :, colour, None, :, :]
            factor_im = link_im[..., :, colour, None, :, :]
        source_re = vec_re[..., colour:colour + 1, :, :, :]
        source_im = vec_im[..., colour:colour + 1, :, :, :]
        out_re = out_re + factor_re * source_re - factor_im * source_im
        out_im = out_im + factor_re * source_im + factor_im * source_re
    return jnp.stack([out_re, out_im], axis=-5)

def smear(vector, gauge):
    summed = (1.0 - 6.0 * KAPPA) * vector
    for direction in range(3):
        one_link = gauge[direction]
        forward = transport(one_link, move(vector, direction, 1), False)
        behind = move(transport(one_link, vector, True), direction, -1)
        summed = summed + KAPPA * (forward + behind)
    return summed

def phases(momenta, z_start, z_count, z_total):
    site_index = jnp.arange(LX * LX, dtype=jnp.int32)
    x_coord = site_index % LX
    y_coord = site_index // LX
    z_coord = z_start + jnp.arange(z_count, dtype=jnp.int32)
    turn_x = momenta[:, 0, None] * x_coord[None] % LX
    turn_y = momenta[:, 1, None] * y_coord[None] % LX
    turn_z = momenta[:, 2, None] * z_coord[None] % z_total
    angles = 2.0 * math.pi * (turn_x.astype(jnp.float32)[:, None, :] / LX + turn_y.astype(jnp.float32)[:, None, :] / LX + turn_z.astype(jnp.float32)[:, :, None] / z_total)
    return (jnp.cos(angles), -jnp.sin(angles))

def contract(smeared, cos_part, sin_part, norm_scale):
    smear_re = smeared[:, 0].astype(jnp.float32)
    smear_im = smeared[:, 1].astype(jnp.float32)
    cos_wide = cos_part[:, None, None, None]
    sin_wide = sin_part[:, None, None, None]
    phased_re = (smear_re[None] * cos_wide - smear_im[None] * sin_wide).astype(jnp.bfloat16)
    phased_im = (smear_re[None] * sin_wide + smear_im[None] * cos_wide).astype(jnp.bfloat16)
    phased = jnp.stack([phased_re, phased_im], axis=2)
    product = jnp.einsum('tlcazs,ptmcbzs->ptlamb', smeared.astype(jnp.float32), phased.astype(jnp.float32), precision=lax.Precision.HIGHEST)
    elem_re = product[:, :, 0, :, 0] + product[:, :, 1, :, 1]
    elem_im = product[:, :, 0, :, 1] - product[:, :, 1, :, 0]
    return norm_scale * jnp.stack([elem_re, elem_im], axis=2)

def reference(eigvecs, gauge_links, perambulators, momenta):
    norm_scale = 1.0 / math.sqrt(3.0 * NZ * LX * LX)
    cos_all, sin_all = phases(momenta, 0, NZ, NZ)

    def per_slice(slice_pair):
        vector, gauge = slice_pair
        vector = vector.reshape(vector.shape[:-2] + (NZ, LX * LX))
        gauge = gauge.reshape(gauge.shape[:-2] + (NZ, LX * LX))
        smeared_nat = smear(vector, gauge).astype(jnp.bfloat16)
        smeared = smeared_nat[None]

        def per_group(group_index):
            cos_group = lax.dynamic_slice_in_dim(cos_all, group_index * op_group, op_group, 0)
            sin_group = lax.dynamic_slice_in_dim(sin_all, group_index * op_group, op_group, 0)
            return contract(smeared, cos_group, sin_group, norm_scale)[:, 0]
        grouped = lax.map(per_group, jnp.arange(NP // op_group, dtype=jnp.int32))
        blocked = smeared_nat.reshape(smeared_nat.shape[:-2] + (NZ * YB, ROWS * LX))
        return (grouped.reshape((NP, 2, NEV, NEV)), blocked)
    raw, smeared_out = lax.map(per_slice, (eigvecs, jnp.moveaxis(gauge_links, 1, 0)))
    elementals = jnp.moveaxis(raw, 0, 1).astype(jnp.bfloat16)
    phi_bf = elementals
    blocks = perambulators.reshape((NT, NT, 2, SPIN * SPIN, NEV, NEV)).astype(jnp.float32)
    tau_re = blocks[:, :, 0]
    tau_im = blocks[:, :, 1]
    high = lax.Precision.HIGHEST

    def per_op(phi_op):
        remote = phi_op.astype(jnp.float32)
        far_re = remote[:, 0]
        far_im = remote[:, 1]
        left_re = jnp.einsum('tnqia,nba->tnqib', tau_re, far_re, precision=high) + jnp.einsum('tnqia,nba->tnqib', tau_im, far_im, precision=high)
        left_im = jnp.einsum('tnqia,nba->tnqib', tau_im, far_re, precision=high) - jnp.einsum('tnqia,nba->tnqib', tau_re, far_im, precision=high)
        left_re = lax.optimization_barrier(left_re.astype(jnp.bfloat16)).astype(jnp.float32)
        left_im = lax.optimization_barrier(left_im.astype(jnp.bfloat16)).astype(jnp.float32)
        right_re = jnp.einsum('tnqib,tnqkb->tnqik', left_re, tau_re, precision=high) + jnp.einsum('tnqib,tnqkb->tnqik', left_im, tau_im, precision=high)
        right_im = jnp.einsum('tnqib,tnqkb->tnqik', left_im, tau_re, precision=high) - jnp.einsum('tnqib,tnqkb->tnqik', left_re, tau_im, precision=high)
        corr_re = jnp.einsum('tab,tnqba->tn', far_re, right_re, precision=high) - jnp.einsum('tab,tnqba->tn', far_im, right_im, precision=high)
        corr_im = jnp.einsum('tab,tnqba->tn', far_re, right_im, precision=high) + jnp.einsum('tab,tnqba->tn', far_im, right_re, precision=high)
        return jnp.stack([corr_re, corr_im]) / NEV
    correlator = lax.map(per_op, phi_bf)
    return (smeared_out, elementals, jnp.moveaxis(correlator, 1, 0))
```

```python
import functools
import math

import jax
import jax.numpy as jnp
from jax import lax
from jax.experimental import pallas as pl
from jax.experimental.pallas import tpu as pltpu
from jax.sharding import PartitionSpec as P

LX = 24
YB = 4
KAPPA = 0.25
VMEM_LIMIT = 40 * 1024 * 1024
NT_DIMS = (((1,), (1,)), ((), ()))


def phases(momenta, z_index, y_start, site_count, z_total):
    site_index = jnp.arange(site_count, dtype=jnp.int32)
    x_coord = site_index % LX
    y_coord = y_start + site_index // LX
    turn_x = momenta[:, 0, None] * x_coord[None] % LX
    turn_y = momenta[:, 1, None] * y_coord[None] % LX
    turn_z = momenta[:, 2, None] * z_index % z_total
    angles = (
        2.0
        * math.pi
        * (
            turn_x.astype(jnp.float32) / LX
            + turn_y.astype(jnp.float32) / LX
            + turn_z.astype(jnp.float32) / z_total
        )
    )
    return jnp.cos(angles), -jnp.sin(angles)


def link_times(link, vector, adjoint):
    real, imag = [], []
    for row in range(3):
        out_re = out_im = None
        for colour in range(3):
            k = colour * 3 + row if adjoint else row * 3 + colour
            a, b = link(k), link(9 + k)
            if adjoint:
                b = -b
            x, y = vector(colour), vector(3 + colour)
            term_re = a * x - b * y
            term_im = a * y + b * x
            out_re = term_re if out_re is None else out_re + term_re
            out_im = term_im if out_im is None else out_im + term_im
        real.append(out_re)
        imag.append(out_im)
    return real + imag


def signed_roll(block, sign_low):
    half = block.shape[-1] // 2
    lane = lax.broadcasted_iota(jnp.int32, block.shape, 1)
    turned = pltpu.roll(block, half, 1)
    low = lane < half
    return jnp.where(low, sign_low * turned, -sign_low * turned)


def smear_kernel(
    norm_scale, v, up, down, u, zb, ra, rb, cs, sn, sm, elem, pad, wide, rows, sums
):
    nev, sites = v.shape[1], v.shape[2]
    lanes = pad.shape[2]
    lane = lax.broadcasted_iota(jnp.int32, (nev, lanes), 1)
    x_coord = lane % LX
    for i in range(6):
        pad[i, :, :sites] = v[i]
        sums[i] = (1.0 - 6.0 * KAPPA) * v[i]

    def add(terms):
        for i in range(6):
            sums[i] = sums[i] + KAPPA * terms[i]

    def link(d):
        return lambda k: u[d, k : k + 1, :]

    def forward_x(i):
        full = pad[i]
        return jnp.where(
            x_coord == LX - 1, pltpu.roll(full, LX - 1, 1), pltpu.roll(full, lanes - 1, 1)
        )[:, :sites]

    def forward_y(i):
        full = pad[i]
        return jnp.where(
            lane >= sites - LX,
            pltpu.roll(rows[i], sites - LX, 1),
            pltpu.roll(full, lanes - LX, 1),
        )[:, :sites]

    for i in range(6):
        rows[i, :, :LX] = ra[i].astype(jnp.float32)
    add(link_times(link(0), forward_x, False))
    add(link_times(link(1), forward_y, False))
    add(link_times(link(2), lambda i: up[i].astype(jnp.float32), False))
    add(link_times(lambda k: zb[k : k + 1, :], lambda i: down[i].astype(jnp.float32), True))
    for i, term in enumerate(link_times(link(0), lambda i: v[i], True)):
        pad[i, :, :sites] = term
    add(
        [
            jnp.where(
                x_coord == 0, pltpu.roll(pad[i], lanes - LX + 1, 1), pltpu.roll(pad[i], 1, 1)
            )[:, :sites]
            for i in range(6)
        ]
    )
    for i, term in enumerate(link_times(link(1), lambda i: v[i], True)):
        pad[i, :, :sites] = term
    for i in range(6):
        rows[i, :, :LX] = rb[i].astype(jnp.float32)
    add(
        [
            jnp.where(lane < LX, rows[i], pltpu.roll(pad[i], LX, 1))[:, :sites]
            for i in range(6)
        ]
    )
    for i in range(6):
        rounded = sums[i].astype(jnp.bfloat16)
        sm[i] = rounded
        wide[i] = rounded.astype(jnp.float32)

    per = 2 if elem.shape[0] % 2 == 0 else 1

    def step(g, carry):
        product = None
        for colour in range(3):
            s_re, s_im = wide[colour], wide[3 + colour]
            parts = []
            for j in range(per):
                cos_row = cs[pl.ds(g * per + j, 1), :]
                sin_row = sn[pl.ds(g * per + j, 1), :]
                parts.append((s_re * cos_row - s_im * sin_row).astype(jnp.bfloat16))
                parts.append((s_re * sin_row + s_im * cos_row).astype(jnp.bfloat16))
            left = jnp.concatenate([sm[colour], sm[3 + colour]], axis=0)
            term = lax.dot_general(
                left, jnp.concatenate(parts, axis=0), NT_DIMS, preferred_element_type=jnp.float32
            )
            product = term if product is None else product + term
        for j in range(per):
            block = product[:, j * 2 * nev : (j + 1) * 2 * nev]
            elem[g * per + j] = norm_scale * (block[:nev] + signed_roll(block[nev:], 1.0))
        return carry

    lax.fori_loop(0, elem.shape[0] // per, step, 0)


def trace_kernel(far, bc, g_re, g_im, out, left, b2, weights):
    ops = far.shape[1]
    nev, width = far.shape[2], far.shape[3]
    pairs = bc.shape[1] // nev
    for p in range(ops):
        block = far[0, p].astype(jnp.float32)
        weights[2 * p * nev : (2 * p + 1) * nev, :] = far[0, p]
        weights[(2 * p + 1) * nev : (2 * p + 2) * nev, :] = signed_roll(block, -1.0).astype(
            jnp.bfloat16
        )
    left[...] = lax.dot_general(
        bc[0], weights[...], NT_DIMS, preferred_element_type=jnp.float32
    ).astype(jnp.bfloat16)
    b2[...] = signed_roll(bc[0].astype(jnp.float32), -1.0).astype(jnp.bfloat16)
    right = None
    for q in range(0, pairs, 2):
        spans = [slice(k * nev, (k + 1) * nev) for k in (q, q + 1)]
        stacked = jnp.concatenate(
            [
                jnp.concatenate([left[s, p * width : (p + 1) * width] for s in spans], axis=1)
                for p in range(ops)
            ],
            axis=0,
        )
        facing = jnp.concatenate(
            [
                jnp.concatenate([bc[0, s, :] for s in spans], axis=1),
                jnp.concatenate([b2[s, :] for s in spans], axis=1),
            ],
            axis=0,
        )
        term = lax.dot_general(stacked, facing, NT_DIMS, preferred_element_type=jnp.float32)
        right = term if right is None else right + term
    for part, g in enumerate((g_re, g_im)):
        for p in range(ops):
            total = jnp.sum(g[p] * right[p * nev : (p + 1) * nev], keepdims=True) / nev
            out[0, part * ops + p : part * ops + p + 1, :] = jnp.broadcast_to(total, (1, width))


def local(eigvecs, gauge_links, perambulators, momenta):
    spaces = lax.axis_size("space")
    z_total = spaces // YB
    nev, sites = eigvecs.shape[3], eigvecs.shape[5]
    block_index = lax.axis_index("space")
    y_block = block_index % YB
    z_index = block_index // YB
    op_count = momenta.shape[0]
    v = eigvecs.reshape(6, nev, sites)
    u = gauge_links.reshape(3, 18, sites)

    def along(value, z_steps, y_steps):
        pairs = []
        for s in range(spaces):
            z, y = s // YB, s % YB
            pairs.append((s, (z + z_steps) % z_total * YB + (y + y_steps) % YB))
        return lax.ppermute(value, "space", pairs)

    narrow = v.astype(jnp.bfloat16)
    up = along(narrow, -1, 0)
    down = up if z_total == 2 else along(narrow, 1, 0)
    zlink = along(u[2], 1, 0)
    edge = jnp.stack(
        link_times(
            lambda k: u[1, k : k + 1, sites - LX :], lambda i: v[i, :, sites - LX :], True
        )
    )
    row_above = along(v[:, :, :LX], 0, -1)
    row_below = along(edge, 0, 1)
    cos_all, sin_all = phases(momenta, z_index, y_block * (sites // LX), sites, z_total)
    t_all = perambulators.shape[1]
    pair_count = perambulators.shape[3] * perambulators.shape[4]
    blocks = perambulators.reshape(t_all, 2, pair_count * nev, nev)
    both = jnp.concatenate([blocks[:, 0], blocks[:, 1]], axis=2)

    lanes = -(-sites // 128) * 128
    smeared, partial_sums = pl.pallas_call(
        functools.partial(smear_kernel, 1.0 / math.sqrt(3.0 * z_total * LX * LX)),
        out_shape=(
            jax.ShapeDtypeStruct((6, nev, sites), jnp.bfloat16),
            jax.ShapeDtypeStruct((op_count, nev, 2 * nev), jnp.float32),
        ),
        scratch_shapes=[
            pltpu.VMEM((6, nev, lanes), jnp.float32),
            pltpu.VMEM((6, nev, sites), jnp.float32),
            pltpu.VMEM((6, nev, lanes), jnp.float32),
            pltpu.VMEM((6, nev, sites), jnp.float32),
        ],
        compiler_params=pltpu.CompilerParams(vmem_limit_bytes=VMEM_LIMIT),
        name="smear",
    )(v, up, down, u, zlink, row_above, row_below, cos_all, sin_all)

    if op_count % spaces == 0:
        own = lax.psum_scatter(partial_sums, "space", scatter_dimension=0, tiled=True)
        own = own.astype(jnp.bfloat16)
        every = lax.all_gather(own, "space", axis=0, tiled=True)
    else:
        every = lax.psum(partial_sums, "space").astype(jnp.bfloat16)
        slots = -(-op_count // spaces)
        ids = jnp.minimum(block_index * slots + jnp.arange(slots), op_count - 1)
        own = jnp.take(every, ids, axis=0)
    ops = own.shape[0]
    far = lax.all_gather(own, "tm", axis=0)
    wide = own.astype(jnp.float32)
    near_re = jnp.swapaxes(wide[:, :, :nev], 1, 2)
    near_im = jnp.swapaxes(wide[:, :, nev:], 1, 2)
    g_re = jnp.concatenate([near_re, -near_im], axis=2)
    g_im = jnp.concatenate([near_im, near_re], axis=2)
    width = 2 * nev
    traces = pl.pallas_call(
        trace_kernel,
        grid=(t_all,),
        out_shape=jax.ShapeDtypeStruct((t_all, 2 * ops, width), jnp.float32),
        in_specs=[
            pl.BlockSpec((1, ops, nev, width), lambda t: (t, 0, 0, 0)),
            pl.BlockSpec((1, pair_count * nev, width), lambda t: (t, 0, 0)),
            pl.BlockSpec((ops, nev, width), lambda t: (0, 0, 0)),
            pl.BlockSpec((ops, nev, width), lambda t: (0, 0, 0)),
        ],
        out_specs=pl.BlockSpec((1, 2 * ops, width), lambda t: (t, 0, 0)),
        scratch_shapes=[
            pltpu.VMEM((pair_count * nev, ops * width), jnp.bfloat16),
            pltpu.VMEM((pair_count * nev, width), jnp.bfloat16),
            pltpu.VMEM((ops * width, width), jnp.bfloat16),
        ],
        compiler_params=pltpu.CompilerParams(vmem_limit_bytes=VMEM_LIMIT),
        name="traces",
    )(far, both, g_re, g_im)
    terms = lax.all_gather(traces[:, :, 0].reshape(t_all, 2, ops), "space", axis=0)
    terms = jnp.transpose(terms, (2, 0, 3, 1)).reshape(2, spaces * ops, t_all)
    correlator = terms[:, :op_count, None, :]
    elementals = jnp.swapaxes(every.reshape(op_count, nev, 2, nev), 1, 2)[:, None]
    return (smeared.reshape(eigvecs.shape), elementals, correlator)


def solution(mesh):
    return jax.shard_map(
        local,
        mesh=mesh,
        in_specs=(
            P("tm", None, None, None, "space", None),
            P(None, "tm", None, None, None, "space", None),
            P("tm", None, None, None, None, None, None),
            P(),
        ),
        out_specs=(
            P("tm", None, None, None, "space", None),
            P(None, "tm", None, None, None),
            P(None, None, "tm", None),
        ),
        check_vma=False,
    )
```

```python
import functools
import math

import jax
import jax.numpy as jnp
from jax import lax
from jax.experimental import pallas as pl
from jax.experimental.pallas import tpu as pltpu
from jax.sharding import PartitionSpec as P

LX = 24
YB = 4
KAPPA = 0.25
VMEM_LIMIT = 40 * 1024 * 1024
NT_DIMS = (((1,), (1,)), ((), ()))


def phases(momenta, z_index, y_start, site_count, z_total):
    site_index = jnp.arange(site_count, dtype=jnp.int32)
    x_coord = site_index % LX
    y_coord = y_start + site_index // LX
    turn_x = momenta[:, 0, None] * x_coord[None] % LX
    turn_y = momenta[:, 1, None] * y_coord[None] % LX
    turn_z = momenta[:, 2, None] * z_index % z_total
    angles = (
        2.0
        * math.pi
        * (
            turn_x.astype(jnp.float32) / LX
            + turn_y.astype(jnp.float32) / LX
            + turn_z.astype(jnp.float32) / z_total
        )
    )
    return jnp.cos(angles), -jnp.sin(angles)


def link_times(link, vector, adjoint):
    real, imag = [], []
    for row in range(3):
        out_re = out_im = None
        for colour in range(3):
            k = colour * 3 + row if adjoint else row * 3 + colour
            a, b = link(k), link(9 + k)
            if adjoint:
                b = -b
            x, y = vector(colour), vector(3 + colour)
            term_re = a * x - b * y
            term_im = a * y + b * x
            out_re = term_re if out_re is None else out_re + term_re
            out_im = term_im if out_im is None else out_im + term_im
        real.append(out_re)
        imag.append(out_im)
    return real + imag


def signed_roll(block, sign_low):
    half = block.shape[-1] // 2
    lane = lax.broadcasted_iota(jnp.int32, block.shape, 1)
    turned = pltpu.roll(block, half, 1)
    low = lane < half
    return jnp.where(low, sign_low * turned, -sign_low * turned)


def smear_kernel(
    norm_scale, v, up, down, u, zb, ra, rb, cs, sn, sm, elem, pad, wide, rows, sums
):
    nev, sites = v.shape[1], v.shape[2]
    lanes = pad.shape[2]
    lane = lax.broadcasted_iota(jnp.int32, (nev, lanes), 1)
    x_coord = lane % LX
    for i in range(6):
        pad[i, :, :sites] = v[i]
        sums[i] = (1.0 - 6.0 * KAPPA) * v[i]

    def add(terms):
        for i in range(6):
            sums[i] = sums[i] + KAPPA * terms[i]

    def link(d):
        return lambda k: u[d, k : k + 1, :]

    def forward_x(i):
        full = pad[i]
        return jnp.where(
            x_coord == LX - 1, pltpu.roll(full, LX - 1, 1), pltpu.roll(full, lanes - 1, 1)
        )[:, :sites]

    def forward_y(i):
        full = pad[i]
        return jnp.where(
            lane >= sites - LX,
            pltpu.roll(rows[i], sites - LX, 1),
            pltpu.roll(full, lanes - LX, 1),
        )[:, :sites]

    for i in range(6):
        rows[i, :, :LX] = ra[i].astype(jnp.float32)
    add(link_times(link(0), forward_x, False))
    add(link_times(link(1), forward_y, False))
    add(link_times(link(2), lambda i: up[i].astype(jnp.float32), False))
    add(link_times(lambda k: zb[k : k + 1, :], lambda i: down[i].astype(jnp.float32), True))
    for i, term in enumerate(link_times(link(0), lambda i: v[i], True)):
        pad[i, :, :sites] = term
    add(
        [
            jnp.where(
                x_coord == 0, pltpu.roll(pad[i], lanes - LX + 1, 1), pltpu.roll(pad[i], 1, 1)
            )[:, :sites]
            for i in range(6)
        ]
    )
    for i, term in enumerate(link_times(link(1), lambda i: v[i], True)):
        pad[i, :, :sites] = term
    for i in range(6):
        rows[i, :, :LX] = rb[i].astype(jnp.float32)
    add(
        [
            jnp.where(lane < LX, rows[i], pltpu.roll(pad[i], LX, 1))[:, :sites]
            for i in range(6)
        ]
    )
    for i in range(6):
        rounded = sums[i].astype(jnp.bfloat16)
        sm[i] = rounded
        wide[i] = rounded.astype(jnp.float32)

    per = 2 if elem.shape[0] % 2 == 0 else 1

    def step(g, carry):
        product = None
        for colour in range(3):
            s_re, s_im = wide[colour], wide[3 + colour]
            parts = []
            for j in range(per):
                cos_row = cs[pl.ds(g * per + j, 1), :]
                sin_row = sn[pl.ds(g * per + j, 1), :]
                parts.append((s_re * cos_row - s_im * sin_row).astype(jnp.bfloat16))
                parts.append((s_re * sin_row + s_im * cos_row).astype(jnp.bfloat16))
            left = jnp.concatenate([sm[colour], sm[3 + colour]], axis=0)
            term = lax.dot_general(
                left, jnp.concatenate(parts, axis=0), NT_DIMS, preferred_element_type=jnp.float32
            )
            product = term if product is None else product + term
        for j in range(per):
            block = product[:, j * 2 * nev : (j + 1) * 2 * nev]
            elem[g * per + j] = norm_scale * (block[:nev] + signed_roll(block[nev:], 1.0))
        return carry

    lax.fori_loop(0, elem.shape[0] // per, step, 0)


def trace_kernel(far, bc, g_re, g_im, out, left, b2, weights):
    ops = far.shape[1]
    nev, width = far.shape[2], far.shape[3]
    pairs = bc.shape[1] // nev
    for p in range(ops):
        block = far[0, p].astype(jnp.float32)
        weights[2 * p * nev : (2 * p + 1) * nev, :] = far[0, p]
        weights[(2 * p + 1) * nev : (2 * p + 2) * nev, :] = signed_roll(block, -1.0).astype(
            jnp.bfloat16
        )
    left[...] = lax.dot_general(
        bc[0], weights[...], NT_DIMS, preferred_element_type=jnp.float32
    ).astype(jnp.bfloat16)
    b2[...] = signed_roll(bc[0].astype(jnp.float32), -1.0).astype(jnp.bfloat16)
    right = None
    for q in range(0, pairs, 2):
        spans = [slice(k * nev, (k + 1) * nev) for k in (q, q + 1)]
        stacked = jnp.concatenate(
            [
                jnp.concatenate([left[s, p * width : (p + 1) * width] for s in spans], axis=1)
                for p in range(ops)
            ],
            axis=0,
        )
        facing = jnp.concatenate(
            [
                jnp.concatenate([bc[0, s, :] for s in spans], axis=1),
                jnp.concatenate([b2[s, :] for s in spans], axis=1),
            ],
            axis=0,
        )
        term = lax.dot_general(stacked, facing, NT_DIMS, preferred_element_type=jnp.float32)
        right = term if right is None else right + term
    for part, g in enumerate((g_re, g_im)):
        for p in range(ops):
            total = jnp.sum(g[p] * right[p * nev : (p + 1) * nev], keepdims=True) / nev
            out[0, part * ops + p : part * ops + p + 1, :] = jnp.broadcast_to(total, (1, width))


def exchange_kernel(
    spaces, slices, partial, bc, every, gathered, inbox, far, left, b2, weights, tile, send, recv
):
    me, mine = lax.axis_index("space"), lax.axis_index("tm")
    ops, nev, width = inbox.shape[1:]
    pairs = bc.shape[1] // nev

    barrier = pltpu.get_barrier_semaphore()
    for d in range(1, spaces):
        pl.semaphore_signal(
            barrier, inc=1, device_id=((me + d) % spaces, mine), device_id_type=pl.DeviceIdType.MESH
        )
    for d in range(1, slices):
        pl.semaphore_signal(
            barrier, inc=1, device_id=(me, (mine + d) % slices), device_id_type=pl.DeviceIdType.MESH
        )
    pl.semaphore_wait(barrier, spaces + slices - 2)

    def to_space(kind, d, source, target):
        return pltpu.make_async_remote_copy(
            src_ref=source,
            dst_ref=target,
            send_sem=send.at[kind, d],
            recv_sem=recv.at[kind, d],
            device_id=((me + d) % spaces, mine),
            device_id_type=pl.DeviceIdType.MESH,
        )

    def to_slice(d, source, target):
        return pltpu.make_async_remote_copy(
            src_ref=source,
            dst_ref=target,
            send_sem=send.at[3, d],
            recv_sem=recv.at[3, d],
            device_id=(me, (mine + d) % slices),
            device_id_type=pl.DeviceIdType.MESH,
        )

    sums = [
        to_space(0, d, partial.at[pl.ds((me + d) % spaces * ops, ops)], inbox.at[d])
        for d in range(1, spaces)
    ]
    for copy in sums:
        copy.start()
    b2[...] = signed_roll_3d(bc)
    total = partial[pl.ds(me * ops, ops)]
    for d, copy in enumerate(sums, 1):
        copy.wait_recv()
        total = total + inbox[d]
    rounded = total.astype(jnp.bfloat16)
    far[mine] = rounded
    every[pl.ds(me * ops, ops)] = rounded
    fars = [to_slice(d, far.at[mine], far.at[mine]) for d in range(1, slices)]
    for copy in fars:
        copy.start()
    shares = [
        to_space(1, d, far.at[mine], every.at[pl.ds(me * ops, ops)]) for d in range(1, spaces)
    ]
    for copy in shares:
        copy.start()

    near = rounded.astype(jnp.float32)
    low = lax.broadcasted_iota(jnp.int32, (nev, width), 1) < nev
    near_re, near_im = [], []
    for p in range(0, ops, 2):
        one, two = near[p], near[p + 1]
        near_re.append(jnp.where(low, one, pltpu.roll(two, nev, 1)))
        near_im.append(jnp.where(low, pltpu.roll(one, nev, 1), two))
    near_re = jnp.concatenate(near_re, axis=1)
    near_im = jnp.concatenate(near_im, axis=1)
    row_id = lax.broadcasted_iota(jnp.int32, (2 * ops, width), 0)
    lane_id = lax.broadcasted_iota(jnp.int32, (2 * ops, width), 1)
    low_row = lax.broadcasted_iota(jnp.int32, (1, width), 1) < nev
    tile[...] = jnp.zeros_like(tile)

    def step(d, carry):
        @pl.when(d > 0)
        def _():
            pltpu.make_async_remote_copy(
                src_ref=far.at[mine],
                dst_ref=far.at[mine],
                send_sem=send.at[3, d],
                recv_sem=recv.at[3, d],
                device_id=(me, (mine + d) % slices),
                device_id_type=pl.DeviceIdType.MESH,
            ).wait_recv()

        t0 = (mine + slices - d) % slices
        for p in range(ops):
            block = far[t0, p]
            weights[2 * p * nev : (2 * p + 1) * nev, :] = block
            weights[(2 * p + 1) * nev : (2 * p + 2) * nev, :] = signed_roll(
                block.astype(jnp.float32), -1.0
            ).astype(jnp.bfloat16)
        left[...] = lax.dot_general(
            bc[t0], weights[...], NT_DIMS, preferred_element_type=jnp.float32
        ).astype(jnp.bfloat16)
        right = None
        for q in range(0, pairs, 2):
            spans = [slice(k * nev, (k + 1) * nev) for k in (q, q + 1)]
            stacked = jnp.concatenate(
                [
                    jnp.concatenate([left[s, p * width : (p + 1) * width] for s in spans], axis=1)
                    for p in range(ops)
                ],
                axis=0,
            )
            facing = jnp.concatenate(
                [
                    jnp.concatenate([bc[t0, s, :] for s in spans], axis=1),
                    jnp.concatenate([b2[t0, s, :] for s in spans], axis=1),
                ],
                axis=0,
            )
            term = lax.dot_general(facing, stacked, NT_DIMS, preferred_element_type=jnp.float32)
            right = term if right is None else right + term
        r_re, r_im = right[:nev], right[nev:]
        rows = (
            jnp.sum(near_re * r_re - near_im * r_im, axis=0, keepdims=True),
            jnp.sum(near_re * r_im + near_im * r_re, axis=0, keepdims=True),
        )
        found = tile[...]
        for part in range(2):
            for p in range(ops):
                half = rows[part][:, p // 2 * width : (p // 2 + 1) * width]
                keep = low_row if p % 2 == 0 else jnp.logical_not(low_row)
                value = jnp.sum(jnp.where(keep, half, 0.0), axis=1, keepdims=True) / nev
                spot = jnp.logical_and(row_id == part * ops + p, lane_id == t0)
                found = jnp.where(spot, value, found)
        tile[...] = found
        return carry

    lax.fori_loop(0, slices, step, 0)
    gathered[me] = tile[...]
    ends = [to_space(2, d, tile, gathered.at[me]) for d in range(1, spaces)]
    for copy in ends:
        copy.start()
    for copy in shares + ends:
        copy.wait_recv()
    for copy in sums + fars + shares + ends:
        copy.wait_send()


def signed_roll_3d(ref):
    block = ref[...].astype(jnp.float32)
    half = block.shape[-1] // 2
    turned = pltpu.roll(block, half, 2)
    low = lax.broadcasted_iota(jnp.int32, block.shape, 2) < half
    return jnp.where(low, -turned, turned).astype(jnp.bfloat16)


def local(eigvecs, gauge_links, perambulators, momenta):
    spaces = lax.axis_size("space")
    z_total = spaces // YB
    nev, sites = eigvecs.shape[3], eigvecs.shape[5]
    block_index = lax.axis_index("space")
    y_block = block_index % YB
    z_index = block_index // YB
    op_count = momenta.shape[0]
    v = eigvecs.reshape(6, nev, sites)
    u = gauge_links.reshape(3, 18, sites)

    def along(value, z_steps, y_steps):
        pairs = []
        for s in range(spaces):
            z, y = s // YB, s % YB
            pairs.append((s, (z + z_steps) % z_total * YB + (y + y_steps) % YB))
        return lax.ppermute(value, "space", pairs)

    narrow = v.astype(jnp.bfloat16)
    up = along(narrow, -1, 0)
    down = up if z_total == 2 else along(narrow, 1, 0)
    zlink = along(u[2], 1, 0)
    edge = jnp.stack(
        link_times(
            lambda k: u[1, k : k + 1, sites - LX :], lambda i: v[i, :, sites - LX :], True
        )
    )
    row_above = along(v[:, :, :LX], 0, -1)
    row_below = along(edge, 0, 1)
    cos_all, sin_all = phases(momenta, z_index, y_block * (sites // LX), sites, z_total)
    t_all = perambulators.shape[1]
    pair_count = perambulators.shape[3] * perambulators.shape[4]
    blocks = perambulators.reshape(t_all, 2, pair_count * nev, nev)
    both = jnp.concatenate([blocks[:, 0], blocks[:, 1]], axis=2)

    lanes = -(-sites // 128) * 128
    smeared, partial_sums = pl.pallas_call(
        functools.partial(smear_kernel, 1.0 / math.sqrt(3.0 * z_total * LX * LX)),
        out_shape=(
            jax.ShapeDtypeStruct((6, nev, sites), jnp.bfloat16),
            jax.ShapeDtypeStruct((op_count, nev, 2 * nev), jnp.float32),
        ),
        scratch_shapes=[
            pltpu.VMEM((6, nev, lanes), jnp.float32),
            pltpu.VMEM((6, nev, sites), jnp.float32),
            pltpu.VMEM((6, nev, lanes), jnp.float32),
            pltpu.VMEM((6, nev, sites), jnp.float32),
        ],
        compiler_params=pltpu.CompilerParams(vmem_limit_bytes=VMEM_LIMIT),
        name="smear",
    )(v, up, down, u, zlink, row_above, row_below, cos_all, sin_all)

    slices = lax.axis_size("tm")
    if op_count % (2 * spaces) == 0 and t_all == slices and pair_count % 2 == 0:
        ops, width = op_count // spaces, 2 * nev
        peers = max(spaces, slices)
        every, gathered = pl.pallas_call(
            functools.partial(exchange_kernel, spaces, slices),
            out_shape=(
                jax.ShapeDtypeStruct((op_count, nev, width), jnp.bfloat16),
                jax.ShapeDtypeStruct((spaces, 2 * ops, width), jnp.float32),
            ),
            in_specs=[pl.BlockSpec(memory_space=pltpu.VMEM)] * 2,
            out_specs=[pl.BlockSpec(memory_space=pltpu.VMEM)] * 2,
            scratch_shapes=[
                pltpu.VMEM((spaces, ops, nev, width), jnp.float32),
                pltpu.VMEM((slices, ops, nev, width), jnp.bfloat16),
                pltpu.VMEM((pair_count * nev, ops * width), jnp.bfloat16),
                pltpu.VMEM((t_all, pair_count * nev, width), jnp.bfloat16),
                pltpu.VMEM((ops * width, width), jnp.bfloat16),
                pltpu.VMEM((2 * ops, width), jnp.float32),
                pltpu.SemaphoreType.DMA((4, peers)),
                pltpu.SemaphoreType.DMA((4, peers)),
            ],
            compiler_params=pltpu.CompilerParams(
                collective_id=0, has_side_effects=True, vmem_limit_bytes=VMEM_LIMIT
            ),
            name="exchange",
        )(partial_sums, both)
        found = gathered[:, :, :t_all].reshape(spaces, 2, ops, t_all)
        correlator = jnp.swapaxes(found, 0, 1).reshape(2, op_count, 1, t_all)
        elementals = jnp.swapaxes(every.reshape(op_count, nev, 2, nev), 1, 2)[:, None]
        return (smeared.reshape(eigvecs.shape), elementals, correlator)

    if op_count % spaces == 0:
        own = lax.psum_scatter(partial_sums, "space", scatter_dimension=0, tiled=True)
        own = own.astype(jnp.bfloat16)
        every = lax.all_gather(own, "space", axis=0, tiled=True)
    else:
        every = lax.psum(partial_sums, "space").astype(jnp.bfloat16)
        slots = -(-op_count // spaces)
        ids = jnp.minimum(block_index * slots + jnp.arange(slots), op_count - 1)
        own = jnp.take(every, ids, axis=0)
    ops = own.shape[0]
    far = lax.all_gather(own, "tm", axis=0)
    wide = own.astype(jnp.float32)
    near_re = jnp.swapaxes(wide[:, :, :nev], 1, 2)
    near_im = jnp.swapaxes(wide[:, :, nev:], 1, 2)
    g_re = jnp.concatenate([near_re, -near_im], axis=2)
    g_im = jnp.concatenate([near_im, near_re], axis=2)
    width = 2 * nev
    traces = pl.pallas_call(
        trace_kernel,
        grid=(t_all,),
        out_shape=jax.ShapeDtypeStruct((t_all, 2 * ops, width), jnp.float32),
        in_specs=[
            pl.BlockSpec((1, ops, nev, width), lambda t: (t, 0, 0, 0)),
            pl.BlockSpec((1, pair_count * nev, width), lambda t: (t, 0, 0)),
            pl.BlockSpec((ops, nev, width), lambda t: (0, 0, 0)),
            pl.BlockSpec((ops, nev, width), lambda t: (0, 0, 0)),
        ],
        out_specs=pl.BlockSpec((1, 2 * ops, width), lambda t: (t, 0, 0)),
        scratch_shapes=[
            pltpu.VMEM((pair_count * nev, ops * width), jnp.bfloat16),
            pltpu.VMEM((pair_count * nev, width), jnp.bfloat16),
            pltpu.VMEM((ops * width, width), jnp.bfloat16),
        ],
        compiler_params=pltpu.CompilerParams(vmem_limit_bytes=VMEM_LIMIT),
        name="traces",
    )(far, both, g_re, g_im)
    terms = lax.all_gather(traces[:, :, 0].reshape(t_all, 2, ops), "space", axis=0)
    terms = jnp.transpose(terms, (2, 0, 3, 1)).reshape(2, spaces * ops, t_all)
    correlator = terms[:, :op_count, None, :]
    elementals = jnp.swapaxes(every.reshape(op_count, nev, 2, nev), 1, 2)[:, None]
    return (smeared.reshape(eigvecs.shape), elementals, correlator)


def solution(mesh):
    return jax.shard_map(
        local,
        mesh=mesh,
        in_specs=(
            P("tm", None, None, None, "space", None),
            P(None, "tm", None, None, None, "space", None),
            P("tm", None, None, None, None, None, None),
            P(),
        ),
        out_specs=(
            P("tm", None, None, None, "space", None),
            P(None, "tm", None, None, None),
            P(None, None, "tm", None),
        ),
        check_vma=False,
    )
```

```python
import functools
import math

import jax
import jax.numpy as jnp
from jax import lax
from jax.experimental import pallas as pl
from jax.experimental.pallas import tpu as pltpu
from jax.sharding import PartitionSpec as P

LX = 24
YB = 4
KAPPA = 0.25
VMEM_LIMIT = 40 * 1024 * 1024
NT_DIMS = (((1,), (1,)), ((), ()))


def phases(momenta, z_index, y_start, site_count, z_total):
    site_index = jnp.arange(site_count, dtype=jnp.int32)
    x_coord = site_index % LX
    y_coord = y_start + site_index // LX
    turn_x = momenta[:, 0, None] * x_coord[None] % LX
    turn_y = momenta[:, 1, None] * y_coord[None] % LX
    turn_z = momenta[:, 2, None] * z_index % z_total
    angles = (
        2.0
        * math.pi
        * (
            turn_x.astype(jnp.float32) / LX
            + turn_y.astype(jnp.float32) / LX
            + turn_z.astype(jnp.float32) / z_total
        )
    )
    return jnp.cos(angles), -jnp.sin(angles)


def link_times(link, vector, adjoint):
    real, imag = [], []
    for row in range(3):
        out_re = out_im = None
        for colour in range(3):
            k = colour * 3 + row if adjoint else row * 3 + colour
            a, b = link(k), link(9 + k)
            if adjoint:
                b = -b
            x, y = vector(colour), vector(3 + colour)
            term_re = a * x - b * y
            term_im = a * y + b * x
            out_re = term_re if out_re is None else out_re + term_re
            out_im = term_im if out_im is None else out_im + term_im
        real.append(out_re)
        imag.append(out_im)
    return real + imag


def signed_roll(block, sign_low):
    half = block.shape[-1] // 2
    lane = lax.broadcasted_iota(jnp.int32, block.shape, 1)
    turned = pltpu.roll(block, half, 1)
    low = lane < half
    return jnp.where(low, sign_low * turned, -sign_low * turned)


def smear_kernel(
    norm_scale, v, up, down, u, zb, ra, rb, cs, sn, sm, elem, pad, wide, rows, sums
):
    nev, sites = v.shape[1], v.shape[2]
    lanes = pad.shape[2]
    lane = lax.broadcasted_iota(jnp.int32, (nev, lanes), 1)
    x_coord = lane % LX
    for i in range(6):
        pad[i, :, :sites] = v[i]
        sums[i] = (1.0 - 6.0 * KAPPA) * v[i]

    def add(terms):
        for i in range(6):
            sums[i] = sums[i] + KAPPA * terms[i]

    def link(d):
        return lambda k: u[d, k : k + 1, :]

    def forward_x(i):
        full = pad[i]
        return jnp.where(
            x_coord == LX - 1, pltpu.roll(full, LX - 1, 1), pltpu.roll(full, lanes - 1, 1)
        )[:, :sites]

    def forward_y(i):
        full = pad[i]
        return jnp.where(
            lane >= sites - LX,
            pltpu.roll(rows[i], sites - LX, 1),
            pltpu.roll(full, lanes - LX, 1),
        )[:, :sites]

    for i in range(6):
        rows[i, :, :LX] = ra[i].astype(jnp.float32)
    add(link_times(link(0), forward_x, False))
    add(link_times(link(1), forward_y, False))
    add(link_times(link(2), lambda i: up[i].astype(jnp.float32), False))
    add(link_times(lambda k: zb[k : k + 1, :], lambda i: down[i].astype(jnp.float32), True))
    for i, term in enumerate(link_times(link(0), lambda i: v[i], True)):
        pad[i, :, :sites] = term
    add(
        [
            jnp.where(
                x_coord == 0, pltpu.roll(pad[i], lanes - LX + 1, 1), pltpu.roll(pad[i], 1, 1)
            )[:, :sites]
            for i in range(6)
        ]
    )
    for i, term in enumerate(link_times(link(1), lambda i: v[i], True)):
        pad[i, :, :sites] = term
    for i in range(6):
        rows[i, :, :LX] = rb[i].astype(jnp.float32)
    add(
        [
            jnp.where(lane < LX, rows[i], pltpu.roll(pad[i], LX, 1))[:, :sites]
            for i in range(6)
        ]
    )
    for i in range(6):
        rounded = sums[i].astype(jnp.bfloat16)
        sm[i] = rounded
        wide[i] = rounded.astype(jnp.float32)

    form_elementals(norm_scale, cs, sn, sm, wide, elem)


def form_elementals(norm_scale, cs, sn, sm, wide, elem):
    nev = wide.shape[1]
    per = 2 if elem.shape[0] % 2 == 0 else 1

    def step(g, carry):
        product = None
        for colour in range(3):
            s_re, s_im = wide[colour], wide[3 + colour]
            parts = []
            for j in range(per):
                cos_row = cs[pl.ds(g * per + j, 1), :]
                sin_row = sn[pl.ds(g * per + j, 1), :]
                parts.append((s_re * cos_row - s_im * sin_row).astype(jnp.bfloat16))
                parts.append((s_re * sin_row + s_im * cos_row).astype(jnp.bfloat16))
            left = jnp.concatenate([sm[colour], sm[3 + colour]], axis=0)
            term = lax.dot_general(
                left, jnp.concatenate(parts, axis=0), NT_DIMS, preferred_element_type=jnp.float32
            )
            product = term if product is None else product + term
        for j in range(per):
            block = product[:, j * 2 * nev : (j + 1) * 2 * nev]
            elem[g * per + j] = norm_scale * (block[:nev] + signed_roll(block[nev:], 1.0))
        return carry

    lax.fori_loop(0, elem.shape[0] // per, step, 0)


def halo_smear_kernel(
    norm_scale, v, u, cs, sn, sm, elem, pad, wide, prod, sums, narrow, other, zb, edge, got, send, recv
):
    me, mine = lax.axis_index("space"), lax.axis_index("tm")
    spaces = lax.axis_size("space")
    nev, sites = v.shape[1], v.shape[2]
    lanes = pad.shape[2]
    z, y = me // YB, me % YB
    across = (me + YB) % spaces
    above = z * YB + (y + 1) % YB
    below = z * YB + (y + YB - 1) % YB
    barrier = pltpu.get_barrier_semaphore()
    for device in (across, above, below):
        pl.semaphore_signal(
            barrier, inc=1, device_id=(device, mine), device_id_type=pl.DeviceIdType.MESH
        )

    def remote(k, source, target, device):
        return pltpu.make_async_remote_copy(
            src_ref=source,
            dst_ref=target,
            send_sem=send.at[k],
            recv_sem=recv.at[k],
            device_id=(device, mine),
            device_id_type=pl.DeviceIdType.MESH,
        )

    for i in range(6):
        narrow[i] = v[i].astype(jnp.bfloat16)
    pl.semaphore_wait(barrier, 3)
    copies = [
        remote(0, narrow, other, across),
        remote(1, u.at[2], zb, across),
        remote(2, edge.at[0], got.at[0], below),
        remote(3, edge.at[1], got.at[1], above),
    ]
    copies[0].start()
    copies[1].start()
    lane = lax.broadcasted_iota(jnp.int32, (nev, lanes), 1)
    x_coord = lane % LX
    last = sites - LX
    pad[...] = jnp.zeros_like(pad)
    prod[...] = jnp.zeros_like(prod)
    for i in range(6):
        pad[i, :, :sites] = v[i]
        sums[i] = (1.0 - 6.0 * KAPPA) * v[i]

    def add(terms):
        for i in range(6):
            sums[i] = sums[i] + KAPPA * terms[i]

    def link(d):
        return lambda k: u[d, k : k + 1, :]

    for i, term in enumerate(link_times(link(1), lambda i: v[i], True)):
        prod[i, :, :sites] = term
    for side, (ref, start) in enumerate(((pad, 0), (prod, last))):
        packed = jnp.zeros((nev, lanes), jnp.float32)
        for i in range(6):
            inside = jnp.logical_and(lane >= i * LX, lane < (i + 1) * LX)
            packed = jnp.where(
                inside, pltpu.roll(ref[i], (i * LX - start + lanes) % lanes, 1), packed
            )
        edge[side] = packed
    copies[2].start()
    copies[3].start()

    def forward_x(i):
        return jnp.where(
            x_coord == LX - 1, pltpu.roll(pad[i], LX - 1, 1), pltpu.roll(pad[i], lanes - 1, 1)
        )[:, :sites]

    def forward_y(i):
        return jnp.where(
            lane >= last,
            pltpu.roll(got[0], (last - i * LX + lanes) % lanes, 1),
            pltpu.roll(pad[i], lanes - LX, 1),
        )[:, :sites]

    def behind_y(i):
        return jnp.where(
            lane < LX,
            pltpu.roll(got[1], (lanes - i * LX) % lanes, 1),
            pltpu.roll(prod[i], LX, 1),
        )[:, :sites]

    add(link_times(link(0), forward_x, False))
    for i, term in enumerate(link_times(link(0), lambda i: v[i], True)):
        wide[i] = term
    copies[2].wait_recv()
    copies[3].wait_recv()
    add(link_times(link(1), forward_y, False))
    add([behind_y(i) for i in range(6)])
    for i in range(6):
        prod[i, :, :sites] = wide[i]
    add(
        [
            jnp.where(
                x_coord == 0, pltpu.roll(prod[i], lanes - LX + 1, 1), pltpu.roll(prod[i], 1, 1)
            )[:, :sites]
            for i in range(6)
        ]
    )
    copies[0].wait_recv()
    copies[1].wait_recv()
    add(link_times(link(2), lambda i: other[i].astype(jnp.float32), False))
    add(link_times(lambda k: zb[k : k + 1, :], lambda i: other[i].astype(jnp.float32), True))
    for i in range(6):
        rounded = sums[i].astype(jnp.bfloat16)
        sm[i] = rounded
        wide[i] = rounded.astype(jnp.float32)
    form_elementals(norm_scale, cs, sn, sm, wide, elem)
    for copy in copies:
        copy.wait_send()


def trace_kernel(far, bc, g_re, g_im, out, left, b2, weights):
    ops = far.shape[1]
    nev, width = far.shape[2], far.shape[3]
    pairs = bc.shape[1] // nev
    for p in range(ops):
        block = far[0, p].astype(jnp.float32)
        weights[2 * p * nev : (2 * p + 1) * nev, :] = far[0, p]
        weights[(2 * p + 1) * nev : (2 * p + 2) * nev, :] = signed_roll(block, -1.0).astype(
            jnp.bfloat16
        )
    left[...] = lax.dot_general(
        bc[0], weights[...], NT_DIMS, preferred_element_type=jnp.float32
    ).astype(jnp.bfloat16)
    b2[...] = signed_roll(bc[0].astype(jnp.float32), -1.0).astype(jnp.bfloat16)
    right = None
    for q in range(0, pairs, 2):
        spans = [slice(k * nev, (k + 1) * nev) for k in (q, q + 1)]
        stacked = jnp.concatenate(
            [
                jnp.concatenate([left[s, p * width : (p + 1) * width] for s in spans], axis=1)
                for p in range(ops)
            ],
            axis=0,
        )
        facing = jnp.concatenate(
            [
                jnp.concatenate([bc[0, s, :] for s in spans], axis=1),
                jnp.concatenate([b2[s, :] for s in spans], axis=1),
            ],
            axis=0,
        )
        term = lax.dot_general(stacked, facing, NT_DIMS, preferred_element_type=jnp.float32)
        right = term if right is None else right + term
    for part, g in enumerate((g_re, g_im)):
        for p in range(ops):
            total = jnp.sum(g[p] * right[p * nev : (p + 1) * nev], keepdims=True) / nev
            out[0, part * ops + p : part * ops + p + 1, :] = jnp.broadcast_to(total, (1, width))


def exchange_kernel(
    spaces, slices, partial, bc, every, gathered, inbox, middle, far, left, b2, weights, tile, send, recv
):
    me, mine = lax.axis_index("space"), lax.axis_index("tm")
    ops, nev, width = inbox.shape[1:]
    pairs = bc.shape[1] // nev

    barrier = pltpu.get_barrier_semaphore()
    for d in range(1, spaces):
        pl.semaphore_signal(
            barrier, inc=1, device_id=((me + d) % spaces, mine), device_id_type=pl.DeviceIdType.MESH
        )
    for d in range(1, slices):
        pl.semaphore_signal(
            barrier, inc=1, device_id=(me, (mine + d) % slices), device_id_type=pl.DeviceIdType.MESH
        )
    pl.semaphore_wait(barrier, spaces + slices - 2)

    depth, side, level = spaces // 2, me % 2, me // 2
    partner = me + 1 - 2 * side

    def remote(kind, d, source, target, device):
        return pltpu.make_async_remote_copy(
            src_ref=source,
            dst_ref=target,
            send_sem=send.at[kind, d],
            recv_sem=recv.at[kind, d],
            device_id=device,
            device_id_type=pl.DeviceIdType.MESH,
        )

    def block_of(ref, device):
        return ref.at[pl.ds(device * ops, ops)]

    order = list(range(depth - 1, -1, -1))
    beside = {}
    for d in order:
        there = (level + d) % depth * 2
        beside[d] = remote(
            0, d, block_of(partial, there + 1 - side), inbox.at[d], (partner, mine)
        )
        beside[d].start()
    b2[...] = signed_roll_3d(bc)
    along = {}
    for d in order:
        beside[d].wait_recv()
        there = (level + d) % depth * 2
        total = partial[pl.ds((there + side) * ops, ops)] + inbox[d]
        if d > 0:
            middle[d] = total
            along[d] = remote(1, d, middle.at[d], inbox.at[depth + d], (there + side, mine))
            along[d].start()
    for d in order[:-1]:
        along[d].wait_recv()
        total = total + inbox[depth + d]
    rounded = total.astype(jnp.bfloat16)
    far[mine] = rounded
    every[pl.ds(me * ops, ops)] = rounded

    def far_copy(d):
        return remote(3, d, far.at[mine], far.at[mine], (me, (mine + d) % slices))

    def share_copy(d):
        there = (level + d) % depth * 2 + side
        return remote(4, d, far.at[mine], block_of(every, me), (there, mine))

    def pass_copy(d):
        origin = (level + depth - d) % depth * 2 + side
        return remote(5, d, block_of(every, origin), block_of(every, origin), (partner, mine))

    for d in range(1, slices):
        far_copy(d).start()
    for d in range(1, depth):
        share_copy(d).start()
    own_pass = remote(5, 0, far.at[mine], block_of(every, me), (partner, mine))
    own_pass.start()

    near = rounded.astype(jnp.float32)
    low = lax.broadcasted_iota(jnp.int32, (nev, width), 1) < nev
    near_re, near_im = [], []
    for p in range(0, ops, 2):
        one, two = near[p], near[p + 1]
        near_re.append(jnp.where(low, one, pltpu.roll(two, nev, 1)))
        near_im.append(jnp.where(low, pltpu.roll(one, nev, 1), two))
    near_re = jnp.concatenate(near_re, axis=1)
    near_im = jnp.concatenate(near_im, axis=1)
    row_id = lax.broadcasted_iota(jnp.int32, (2 * ops, width), 0)
    lane_id = lax.broadcasted_iota(jnp.int32, (2 * ops, width), 1)
    low_row = lax.broadcasted_iota(jnp.int32, (1, width), 1) < nev
    tile[...] = jnp.zeros_like(tile)

    def step(d, carry):
        @pl.when(d > 0)
        def _():
            far_copy(d).wait_recv()

        @pl.when(jnp.logical_and(d > 0, d < depth))
        def _():
            share_copy(d).wait_recv()
            pass_copy(d).start()

        t0 = (mine + slices - d) % slices
        for p in range(ops):
            block = far[t0, p]
            weights[2 * p * nev : (2 * p + 1) * nev, :] = block
            weights[(2 * p + 1) * nev : (2 * p + 2) * nev, :] = signed_roll(
                block.astype(jnp.float32), -1.0
            ).astype(jnp.bfloat16)
        left[...] = lax.dot_general(
            bc[t0], weights[...], NT_DIMS, preferred_element_type=jnp.float32
        ).astype(jnp.bfloat16)
        right = None
        for q in range(0, pairs, 2):
            spans = [slice(k * nev, (k + 1) * nev) for k in (q, q + 1)]
            stacked = jnp.concatenate(
                [
                    jnp.concatenate([left[s, p * width : (p + 1) * width] for s in spans], axis=1)
                    for p in range(ops)
                ],
                axis=0,
            )
            facing = jnp.concatenate(
                [
                    jnp.concatenate([bc[t0, s, :] for s in spans], axis=1),
                    jnp.concatenate([b2[t0, s, :] for s in spans], axis=1),
                ],
                axis=0,
            )
            term = lax.dot_general(facing, stacked, NT_DIMS, preferred_element_type=jnp.float32)
            right = term if right is None else right + term
        r_re, r_im = right[:nev], right[nev:]
        rows = (
            jnp.sum(near_re * r_re - near_im * r_im, axis=0, keepdims=True),
            jnp.sum(near_re * r_im + near_im * r_re, axis=0, keepdims=True),
        )
        found = tile[...]
        for part in range(2):
            for p in range(ops):
                half = rows[part][:, p // 2 * width : (p // 2 + 1) * width]
                keep = low_row if p % 2 == 0 else jnp.logical_not(low_row)
                value = jnp.sum(jnp.where(keep, half, 0.0), axis=1, keepdims=True) / nev
                spot = jnp.logical_and(row_id == part * ops + p, lane_id == t0)
                found = jnp.where(spot, value, found)
        tile[...] = found
        return carry

    lax.fori_loop(0, slices, step, 0)
    gathered[me] = tile[...]
    ends = [
        remote(2, d, tile, gathered.at[me], ((me + d) % spaces, mine)) for d in range(1, spaces)
    ]
    for copy in ends:
        copy.start()
    passes = [own_pass] + [pass_copy(d) for d in range(1, depth)]
    for copy in passes + ends:
        copy.wait_recv()
    shares = [share_copy(d) for d in range(1, depth)]
    fars = [far_copy(d) for d in range(1, slices)]
    for copy in list(beside.values()) + list(along.values()) + fars + shares + passes + ends:
        copy.wait_send()


def signed_roll_3d(ref):
    block = ref[...].astype(jnp.float32)
    half = block.shape[-1] // 2
    turned = pltpu.roll(block, half, 2)
    low = lax.broadcasted_iota(jnp.int32, block.shape, 2) < half
    return jnp.where(low, -turned, turned).astype(jnp.bfloat16)


def local(eigvecs, gauge_links, perambulators, momenta):
    spaces = lax.axis_size("space")
    z_total = spaces // YB
    nev, sites = eigvecs.shape[3], eigvecs.shape[5]
    block_index = lax.axis_index("space")
    y_block = block_index % YB
    z_index = block_index // YB
    op_count = momenta.shape[0]
    v = eigvecs.reshape(6, nev, sites)
    u = gauge_links.reshape(3, 18, sites)

    def along(value, z_steps, y_steps):
        pairs = []
        for s in range(spaces):
            z, y = s // YB, s % YB
            pairs.append((s, (z + z_steps) % z_total * YB + (y + y_steps) % YB))
        return lax.ppermute(value, "space", pairs)

    cos_all, sin_all = phases(momenta, z_index, y_block * (sites // LX), sites, z_total)
    t_all = perambulators.shape[1]
    pair_count = perambulators.shape[3] * perambulators.shape[4]
    blocks = perambulators.reshape(t_all, 2, pair_count * nev, nev)
    both = jnp.concatenate([blocks[:, 0], blocks[:, 1]], axis=2)

    lanes = -(-sites // 128) * 128
    norm_scale = 1.0 / math.sqrt(3.0 * z_total * LX * LX)
    if z_total == 2 and lanes >= 6 * LX:
        smeared, partial_sums = pl.pallas_call(
            functools.partial(halo_smear_kernel, norm_scale),
            out_shape=(
                jax.ShapeDtypeStruct((6, nev, sites), jnp.bfloat16),
                jax.ShapeDtypeStruct((op_count, nev, 2 * nev), jnp.float32),
            ),
            in_specs=[pl.BlockSpec(memory_space=pltpu.VMEM)] * 4,
            out_specs=[pl.BlockSpec(memory_space=pltpu.VMEM)] * 2,
            scratch_shapes=[
                pltpu.VMEM((6, nev, lanes), jnp.float32),
                pltpu.VMEM((6, nev, sites), jnp.float32),
                pltpu.VMEM((6, nev, lanes), jnp.float32),
                pltpu.VMEM((6, nev, sites), jnp.float32),
                pltpu.VMEM((6, nev, sites), jnp.bfloat16),
                pltpu.VMEM((6, nev, sites), jnp.bfloat16),
                pltpu.VMEM((18, sites), jnp.float32),
                pltpu.VMEM((2, nev, lanes), jnp.float32),
                pltpu.VMEM((2, nev, lanes), jnp.float32),
                pltpu.SemaphoreType.DMA((4,)),
                pltpu.SemaphoreType.DMA((4,)),
            ],
            compiler_params=pltpu.CompilerParams(
                collective_id=1, has_side_effects=True, vmem_limit_bytes=VMEM_LIMIT
            ),
            name="halo_smear",
        )(v, u, cos_all, sin_all)
    else:
        narrow = v.astype(jnp.bfloat16)
        up = along(narrow, -1, 0)
        down = up if z_total == 2 else along(narrow, 1, 0)
        zlink = along(u[2], 1, 0)
        edge = jnp.stack(
            link_times(
                lambda k: u[1, k : k + 1, sites - LX :], lambda i: v[i, :, sites - LX :], True
            )
        )
        row_above = along(v[:, :, :LX], 0, -1)
        row_below = along(edge, 0, 1)
        smeared, partial_sums = pl.pallas_call(
            functools.partial(smear_kernel, 1.0 / math.sqrt(3.0 * z_total * LX * LX)),
            out_shape=(
                jax.ShapeDtypeStruct((6, nev, sites), jnp.bfloat16),
                jax.ShapeDtypeStruct((op_count, nev, 2 * nev), jnp.float32),
            ),
            scratch_shapes=[
                pltpu.VMEM((6, nev, lanes), jnp.float32),
                pltpu.VMEM((6, nev, sites), jnp.float32),
                pltpu.VMEM((6, nev, lanes), jnp.float32),
                pltpu.VMEM((6, nev, sites), jnp.float32),
            ],
            compiler_params=pltpu.CompilerParams(vmem_limit_bytes=VMEM_LIMIT),
            name="smear",
        )(v, up, down, u, zlink, row_above, row_below, cos_all, sin_all)

    slices = lax.axis_size("tm")
    if op_count % (2 * spaces) == 0 and t_all == slices and pair_count % 2 == 0 and spaces <= 2 * slices:
        ops, width = op_count // spaces, 2 * nev
        peers = max(spaces, slices)
        every, gathered = pl.pallas_call(
            functools.partial(exchange_kernel, spaces, slices),
            out_shape=(
                jax.ShapeDtypeStruct((op_count, nev, width), jnp.bfloat16),
                jax.ShapeDtypeStruct((spaces, 2 * ops, width), jnp.float32),
            ),
            in_specs=[pl.BlockSpec(memory_space=pltpu.VMEM)] * 2,
            out_specs=[pl.BlockSpec(memory_space=pltpu.VMEM)] * 2,
            scratch_shapes=[
                pltpu.VMEM((spaces, ops, nev, width), jnp.float32),
                pltpu.VMEM((spaces // 2, ops, nev, width), jnp.float32),
                pltpu.VMEM((slices, ops, nev, width), jnp.bfloat16),
                pltpu.VMEM((pair_count * nev, ops * width), jnp.bfloat16),
                pltpu.VMEM((t_all, pair_count * nev, width), jnp.bfloat16),
                pltpu.VMEM((ops * width, width), jnp.bfloat16),
                pltpu.VMEM((2 * ops, width), jnp.float32),
                pltpu.SemaphoreType.DMA((6, peers)),
                pltpu.SemaphoreType.DMA((6, peers)),
            ],
            compiler_params=pltpu.CompilerParams(
                collective_id=0, has_side_effects=True, vmem_limit_bytes=VMEM_LIMIT
            ),
            name="exchange",
        )(partial_sums, both)
        found = gathered[:, :, :t_all].reshape(spaces, 2, ops, t_all)
        correlator = jnp.swapaxes(found, 0, 1).reshape(2, op_count, 1, t_all)
        elementals = jnp.swapaxes(every.reshape(op_count, nev, 2, nev), 1, 2)[:, None]
        return (smeared.reshape(eigvecs.shape), elementals, correlator)

    if op_count % spaces == 0:
        own = lax.psum_scatter(partial_sums, "space", scatter_dimension=0, tiled=True)
        own = own.astype(jnp.bfloat16)
        every = lax.all_gather(own, "space", axis=0, tiled=True)
    else:
        every = lax.psum(partial_sums, "space").astype(jnp.bfloat16)
        slots = -(-op_count // spaces)
        ids = jnp.minimum(block_index * slots + jnp.arange(slots), op_count - 1)
        own = jnp.take(every, ids, axis=0)
    ops = own.shape[0]
    far = lax.all_gather(own, "tm", axis=0)
    wide = own.astype(jnp.float32)
    near_re = jnp.swapaxes(wide[:, :, :nev], 1, 2)
    near_im = jnp.swapaxes(wide[:, :, nev:], 1, 2)
    g_re = jnp.concatenate([near_re, -near_im], axis=2)
    g_im = jnp.concatenate([near_im, near_re], axis=2)
    width = 2 * nev
    traces = pl.pallas_call(
        trace_kernel,
        grid=(t_all,),
        out_shape=jax.ShapeDtypeStruct((t_all, 2 * ops, width), jnp.float32),
        in_specs=[
            pl.BlockSpec((1, ops, nev, width), lambda t: (t, 0, 0, 0)),
            pl.BlockSpec((1, pair_count * nev, width), lambda t: (t, 0, 0)),
            pl.BlockSpec((ops, nev, width), lambda t: (0, 0, 0)),
            pl.BlockSpec((ops, nev, width), lambda t: (0, 0, 0)),
        ],
        out_specs=pl.BlockSpec((1, 2 * ops, width), lambda t: (t, 0, 0)),
        scratch_shapes=[
            pltpu.VMEM((pair_count * nev, ops * width), jnp.bfloat16),
            pltpu.VMEM((pair_count * nev, width), jnp.bfloat16),
            pltpu.VMEM((ops * width, width), jnp.bfloat16),
        ],
        compiler_params=pltpu.CompilerParams(vmem_limit_bytes=VMEM_LIMIT),
        name="traces",
    )(far, both, g_re, g_im)
    terms = lax.all_gather(traces[:, :, 0].reshape(t_all, 2, ops), "space", axis=0)
    terms = jnp.transpose(terms, (2, 0, 3, 1)).reshape(2, spaces * ops, t_all)
    correlator = terms[:, :op_count, None, :]
    elementals = jnp.swapaxes(every.reshape(op_count, nev, 2, nev), 1, 2)[:, None]
    return (smeared.reshape(eigvecs.shape), elementals, correlator)


def solution(mesh):
    return jax.shard_map(
        local,
        mesh=mesh,
        in_specs=(
            P("tm", None, None, None, "space", None),
            P(None, "tm", None, None, None, "space", None),
            P("tm", None, None, None, None, None, None),
            P(),
        ),
        out_specs=(
            P("tm", None, None, None, "space", None),
            P(None, "tm", None, None, None),
            P(None, None, "tm", None),
        ),
        check_vma=False,
    )
```

```python
import functools
import math

import jax
import jax.numpy as jnp
from jax import lax
from jax.experimental import pallas as pl
from jax.experimental.pallas import tpu as pltpu
from jax.sharding import PartitionSpec as P

LX = 24
YB = 4
KAPPA = 0.25
VMEM_LIMIT = 40 * 1024 * 1024
NT_DIMS = (((1,), (1,)), ((), ()))


def phases(momenta, z_index, y_start, site_count, z_total):
    site_index = jnp.arange(site_count, dtype=jnp.int32)
    x_coord = site_index % LX
    y_coord = y_start + site_index // LX
    turn_x = momenta[:, 0, None] * x_coord[None] % LX
    turn_y = momenta[:, 1, None] * y_coord[None] % LX
    turn_z = momenta[:, 2, None] * z_index % z_total
    angles = (
        2.0
        * math.pi
        * (
            turn_x.astype(jnp.float32) / LX
            + turn_y.astype(jnp.float32) / LX
            + turn_z.astype(jnp.float32) / z_total
        )
    )
    return jnp.cos(angles), -jnp.sin(angles)


def link_times(link, vector, adjoint):
    real, imag = [], []
    for row in range(3):
        out_re = out_im = None
        for colour in range(3):
            k = colour * 3 + row if adjoint else row * 3 + colour
            a, b = link(k), link(9 + k)
            if adjoint:
                b = -b
            x, y = vector(colour), vector(3 + colour)
            term_re = a * x - b * y
            term_im = a * y + b * x
            out_re = term_re if out_re is None else out_re + term_re
            out_im = term_im if out_im is None else out_im + term_im
        real.append(out_re)
        imag.append(out_im)
    return real + imag


def signed_roll(block, sign_low):
    half = block.shape[-1] // 2
    lane = lax.broadcasted_iota(jnp.int32, block.shape, 1)
    turned = pltpu.roll(block, half, 1)
    low = lane < half
    return jnp.where(low, sign_low * turned, -sign_low * turned)


def smear_kernel(
    norm_scale, v, up, down, u, zb, ra, rb, cs, sn, sm, elem, pad, wide, rows, sums
):
    nev, sites = v.shape[1], v.shape[2]
    lanes = pad.shape[2]
    lane = lax.broadcasted_iota(jnp.int32, (nev, lanes), 1)
    x_coord = lane % LX
    for i in range(6):
        pad[i, :, :sites] = v[i]
        sums[i] = (1.0 - 6.0 * KAPPA) * v[i]

    def add(terms):
        for i in range(6):
            sums[i] = sums[i] + KAPPA * terms[i]

    def link(d):
        return lambda k: u[d, k : k + 1, :]

    def forward_x(i):
        full = pad[i]
        return jnp.where(
            x_coord == LX - 1, pltpu.roll(full, LX - 1, 1), pltpu.roll(full, lanes - 1, 1)
        )[:, :sites]

    def forward_y(i):
        full = pad[i]
        return jnp.where(
            lane >= sites - LX,
            pltpu.roll(rows[i], sites - LX, 1),
            pltpu.roll(full, lanes - LX, 1),
        )[:, :sites]

    for i in range(6):
        rows[i, :, :LX] = ra[i].astype(jnp.float32)
    add(link_times(link(0), forward_x, False))
    add(link_times(link(1), forward_y, False))
    add(link_times(link(2), lambda i: up[i].astype(jnp.float32), False))
    add(link_times(lambda k: zb[k : k + 1, :], lambda i: down[i].astype(jnp.float32), True))
    for i, term in enumerate(link_times(link(0), lambda i: v[i], True)):
        pad[i, :, :sites] = term
    add(
        [
            jnp.where(
                x_coord == 0, pltpu.roll(pad[i], lanes - LX + 1, 1), pltpu.roll(pad[i], 1, 1)
            )[:, :sites]
            for i in range(6)
        ]
    )
    for i, term in enumerate(link_times(link(1), lambda i: v[i], True)):
        pad[i, :, :sites] = term
    for i in range(6):
        rows[i, :, :LX] = rb[i].astype(jnp.float32)
    add(
        [
            jnp.where(lane < LX, rows[i], pltpu.roll(pad[i], LX, 1))[:, :sites]
            for i in range(6)
        ]
    )
    for i in range(6):
        rounded = sums[i].astype(jnp.bfloat16)
        sm[i] = rounded
        wide[i] = rounded.astype(jnp.float32)

    form_elementals(norm_scale, cs, sn, sm, wide, elem, 0, elem.shape[0])


def form_elementals(norm_scale, cs, sn, sm, wide, elem, first, count):
    nev = wide.shape[1]
    per = 2 if count % 2 == 0 else 1

    def step(k, carry):
        start = first + k * per
        product = None
        for colour in range(3):
            s_re, s_im = wide[colour], wide[3 + colour]
            parts = []
            for j in range(per):
                cos_row = cs[pl.ds(start + j, 1), :]
                sin_row = sn[pl.ds(start + j, 1), :]
                parts.append((s_re * cos_row - s_im * sin_row).astype(jnp.bfloat16))
                parts.append((s_re * sin_row + s_im * cos_row).astype(jnp.bfloat16))
            left = jnp.concatenate([sm[colour], sm[3 + colour]], axis=0)
            term = lax.dot_general(
                left, jnp.concatenate(parts, axis=0), NT_DIMS, preferred_element_type=jnp.float32
            )
            product = term if product is None else product + term
        for j in range(per):
            block = product[:, j * 2 * nev : (j + 1) * 2 * nev]
            elem[start + j] = norm_scale * (block[:nev] + signed_roll(block[nev:], 1.0))
        return carry

    lax.fori_loop(0, count // per, step, 0)


def whole_kernel(
    spaces,
    slices,
    norm_scale,
    v,
    u,
    cs,
    sn,
    bc,
    sm,
    every,
    gathered,
    pad,
    wide,
    prod,
    sums,
    narrow,
    other,
    zb,
    edge,
    got,
    send,
    recv,
    elem,
    *rest,
):
    me, mine = lax.axis_index("space"), lax.axis_index("tm")
    nev, sites = v.shape[1], v.shape[2]
    lanes = pad.shape[2]
    z, y = me // YB, me % YB
    across = (me + YB) % spaces
    above = z * YB + (y + 1) % YB
    below = z * YB + (y + YB - 1) % YB
    barrier = pltpu.get_barrier_semaphore()
    for d in range(1, spaces):
        pl.semaphore_signal(
            barrier, inc=1, device_id=((me + d) % spaces, mine), device_id_type=pl.DeviceIdType.MESH
        )
    for d in range(1, slices):
        pl.semaphore_signal(
            barrier, inc=1, device_id=(me, (mine + d) % slices), device_id_type=pl.DeviceIdType.MESH
        )

    def remote(k, source, target, device):
        return pltpu.make_async_remote_copy(
            src_ref=source,
            dst_ref=target,
            send_sem=send.at[k],
            recv_sem=recv.at[k],
            device_id=(device, mine),
            device_id_type=pl.DeviceIdType.MESH,
        )

    for i in range(6):
        narrow[i] = v[i].astype(jnp.bfloat16)
    pl.semaphore_wait(barrier, spaces + slices - 2)
    copies = [
        remote(0, narrow, other, across),
        remote(1, u.at[2], zb, across),
        remote(2, edge.at[0], got.at[0], below),
        remote(3, edge.at[1], got.at[1], above),
    ]
    copies[0].start()
    copies[1].start()
    lane = lax.broadcasted_iota(jnp.int32, (nev, lanes), 1)
    x_coord = lane % LX
    last = sites - LX
    pad[...] = jnp.zeros_like(pad)
    prod[...] = jnp.zeros_like(prod)
    for i in range(6):
        pad[i, :, :sites] = v[i]
        sums[i] = (1.0 - 6.0 * KAPPA) * v[i]

    def add(terms):
        for i in range(6):
            sums[i] = sums[i] + KAPPA * terms[i]

    def link(d):
        return lambda k: u[d, k : k + 1, :]

    for i, term in enumerate(link_times(link(1), lambda i: v[i], True)):
        prod[i, :, :sites] = term
    for side, (ref, start) in enumerate(((pad, 0), (prod, last))):
        packed = jnp.zeros((nev, lanes), jnp.float32)
        for i in range(6):
            inside = jnp.logical_and(lane >= i * LX, lane < (i + 1) * LX)
            packed = jnp.where(
                inside, pltpu.roll(ref[i], (i * LX - start + lanes) % lanes, 1), packed
            )
        edge[side] = packed
    copies[2].start()
    copies[3].start()

    def forward_x(i):
        return jnp.where(
            x_coord == LX - 1, pltpu.roll(pad[i], LX - 1, 1), pltpu.roll(pad[i], lanes - 1, 1)
        )[:, :sites]

    def forward_y(i):
        return jnp.where(
            lane >= last,
            pltpu.roll(got[0], (last - i * LX + lanes) % lanes, 1),
            pltpu.roll(pad[i], lanes - LX, 1),
        )[:, :sites]

    def behind_y(i):
        return jnp.where(
            lane < LX,
            pltpu.roll(got[1], (lanes - i * LX) % lanes, 1),
            pltpu.roll(prod[i], LX, 1),
        )[:, :sites]

    add(link_times(link(0), forward_x, False))
    for i, term in enumerate(link_times(link(0), lambda i: v[i], True)):
        wide[i] = term
    copies[2].wait_recv()
    copies[3].wait_recv()
    add(link_times(link(1), forward_y, False))
    add([behind_y(i) for i in range(6)])
    for i in range(6):
        prod[i, :, :sites] = wide[i]
    add(
        [
            jnp.where(
                x_coord == 0, pltpu.roll(prod[i], lanes - LX + 1, 1), pltpu.roll(prod[i], 1, 1)
            )[:, :sites]
            for i in range(6)
        ]
    )
    copies[0].wait_recv()
    copies[1].wait_recv()
    add(link_times(link(2), lambda i: other[i].astype(jnp.float32), False))
    add(link_times(lambda k: zb[k : k + 1, :], lambda i: other[i].astype(jnp.float32), True))
    for i in range(6):
        rounded = sums[i].astype(jnp.bfloat16)
        sm[i] = rounded
        wide[i] = rounded.astype(jnp.float32)

    ops = elem.shape[0] // spaces

    def form(device):
        form_elementals(norm_scale, cs, sn, sm, wide, elem, device * ops, ops)

    exchange(form, spaces, slices, elem, bc, every, gathered, *rest)
    for copy in copies:
        copy.wait_send()


def trace_kernel(far, bc, g_re, g_im, out, left, b2, weights):
    ops = far.shape[1]
    nev, width = far.shape[2], far.shape[3]
    pairs = bc.shape[1] // nev
    for p in range(ops):
        block = far[0, p].astype(jnp.float32)
        weights[2 * p * nev : (2 * p + 1) * nev, :] = far[0, p]
        weights[(2 * p + 1) * nev : (2 * p + 2) * nev, :] = signed_roll(block, -1.0).astype(
            jnp.bfloat16
        )
    left[...] = lax.dot_general(
        bc[0], weights[...], NT_DIMS, preferred_element_type=jnp.float32
    ).astype(jnp.bfloat16)
    b2[...] = signed_roll(bc[0].astype(jnp.float32), -1.0).astype(jnp.bfloat16)
    right = None
    for q in range(0, pairs, 2):
        spans = [slice(k * nev, (k + 1) * nev) for k in (q, q + 1)]
        stacked = jnp.concatenate(
            [
                jnp.concatenate([left[s, p * width : (p + 1) * width] for s in spans], axis=1)
                for p in range(ops)
            ],
            axis=0,
        )
        facing = jnp.concatenate(
            [
                jnp.concatenate([bc[0, s, :] for s in spans], axis=1),
                jnp.concatenate([b2[s, :] for s in spans], axis=1),
            ],
            axis=0,
        )
        term = lax.dot_general(stacked, facing, NT_DIMS, preferred_element_type=jnp.float32)
        right = term if right is None else right + term
    for part, g in enumerate((g_re, g_im)):
        for p in range(ops):
            total = jnp.sum(g[p] * right[p * nev : (p + 1) * nev], keepdims=True) / nev
            out[0, part * ops + p : part * ops + p + 1, :] = jnp.broadcast_to(total, (1, width))


def exchange(
    form, spaces, slices, partial, bc, every, gathered, inbox, middle, far, left, b2, weights, tile, send, recv
):
    me, mine = lax.axis_index("space"), lax.axis_index("tm")
    ops, nev, width = inbox.shape[1:]
    pairs = bc.shape[1] // nev

    depth, side, level = spaces // 2, me % 2, me // 2
    partner = me + 1 - 2 * side

    def remote(kind, d, source, target, device):
        return pltpu.make_async_remote_copy(
            src_ref=source,
            dst_ref=target,
            send_sem=send.at[kind, d],
            recv_sem=recv.at[kind, d],
            device_id=device,
            device_id_type=pl.DeviceIdType.MESH,
        )

    def block_of(ref, device):
        return ref.at[pl.ds(device * ops, ops)]

    order = list(range(depth - 1, -1, -1))
    beside, along = {}, {}

    def hand_on(d):
        beside[d].wait_recv()
        there = (level + d) % depth * 2
        total = partial[pl.ds((there + side) * ops, ops)] + inbox[d]
        if d > 0:
            middle[d] = total
            along[d] = remote(1, d, middle.at[d], inbox.at[depth + d], (there + side, mine))
            along[d].start()
        return total

    for k, d in enumerate(order):
        there = (level + d) % depth * 2
        form(there + 1 - side)
        beside[d] = remote(
            0, d, block_of(partial, there + 1 - side), inbox.at[d], (partner, mine)
        )
        beside[d].start()
        form(there + side)
        if k > 0:
            hand_on(order[k - 1])
    b2[...] = signed_roll_3d(bc)
    total = hand_on(0)
    for d in order[:-1]:
        along[d].wait_recv()
        total = total + inbox[depth + d]
    rounded = total.astype(jnp.bfloat16)
    far[mine] = rounded
    every[pl.ds(me * ops, ops)] = rounded

    def far_copy(d):
        return remote(3, d, far.at[mine], far.at[mine], (me, (mine + d) % slices))

    def share_copy(d):
        there = (level + d) % depth * 2 + side
        return remote(4, d, far.at[mine], block_of(every, me), (there, mine))

    def pass_copy(d):
        origin = (level + depth - d) % depth * 2 + side
        return remote(5, d, block_of(every, origin), block_of(every, origin), (partner, mine))

    for d in range(1, slices):
        far_copy(d).start()
    for d in range(1, depth):
        share_copy(d).start()
    own_pass = remote(5, 0, far.at[mine], block_of(every, me), (partner, mine))
    own_pass.start()

    near = rounded.astype(jnp.float32)
    low = lax.broadcasted_iota(jnp.int32, (nev, width), 1) < nev
    near_re, near_im = [], []
    for p in range(0, ops, 2):
        one, two = near[p], near[p + 1]
        near_re.append(jnp.where(low, one, pltpu.roll(two, nev, 1)))
        near_im.append(jnp.where(low, pltpu.roll(one, nev, 1), two))
    near_re = jnp.concatenate(near_re, axis=1)
    near_im = jnp.concatenate(near_im, axis=1)
    row_id = lax.broadcasted_iota(jnp.int32, (2 * ops, width), 0)
    lane_id = lax.broadcasted_iota(jnp.int32, (2 * ops, width), 1)
    low_row = lax.broadcasted_iota(jnp.int32, (1, width), 1) < nev
    tile[...] = jnp.zeros_like(tile)

    def step(d, carry):
        @pl.when(d > 0)
        def _():
            far_copy(d).wait_recv()

        @pl.when(jnp.logical_and(d > 0, d < depth))
        def _():
            share_copy(d).wait_recv()
            pass_copy(d).start()

        t0 = (mine + slices - d) % slices
        for p in range(ops):
            block = far[t0, p]
            weights[2 * p * nev : (2 * p + 1) * nev, :] = block
            weights[(2 * p + 1) * nev : (2 * p + 2) * nev, :] = signed_roll(
                block.astype(jnp.float32), -1.0
            ).astype(jnp.bfloat16)
        left[...] = lax.dot_general(
            bc[t0], weights[...], NT_DIMS, preferred_element_type=jnp.float32
        ).astype(jnp.bfloat16)
        right = None
        for q in range(0, pairs, 2):
            spans = [slice(k * nev, (k + 1) * nev) for k in (q, q + 1)]
            stacked = jnp.concatenate(
                [
                    jnp.concatenate([left[s, p * width : (p + 1) * width] for s in spans], axis=1)
                    for p in range(ops)
                ],
                axis=0,
            )
            facing = jnp.concatenate(
                [
                    jnp.concatenate([bc[t0, s, :] for s in spans], axis=1),
                    jnp.concatenate([b2[t0, s, :] for s in spans], axis=1),
                ],
                axis=0,
            )
            term = lax.dot_general(facing, stacked, NT_DIMS, preferred_element_type=jnp.float32)
            right = term if right is None else right + term
        r_re, r_im = right[:nev], right[nev:]
        rows = (
            jnp.sum(near_re * r_re - near_im * r_im, axis=0, keepdims=True),
            jnp.sum(near_re * r_im + near_im * r_re, axis=0, keepdims=True),
        )
        found = tile[...]
        for part in range(2):
            for p in range(ops):
                half = rows[part][:, p // 2 * width : (p // 2 + 1) * width]
                keep = low_row if p % 2 == 0 else jnp.logical_not(low_row)
                value = jnp.sum(jnp.where(keep, half, 0.0), axis=1, keepdims=True) / nev
                spot = jnp.logical_and(row_id == part * ops + p, lane_id == t0)
                found = jnp.where(spot, value, found)
        tile[...] = found
        return carry

    lax.fori_loop(0, slices, step, 0)
    gathered[me] = tile[...]
    ends = [
        remote(2, d, tile, gathered.at[me], ((me + d) % spaces, mine)) for d in range(1, spaces)
    ]
    for copy in ends:
        copy.start()
    passes = [own_pass] + [pass_copy(d) for d in range(1, depth)]
    for copy in passes + ends:
        copy.wait_recv()
    shares = [share_copy(d) for d in range(1, depth)]
    fars = [far_copy(d) for d in range(1, slices)]
    for copy in list(beside.values()) + list(along.values()) + fars + shares + passes + ends:
        copy.wait_send()


def signed_roll_3d(ref):
    block = ref[...].astype(jnp.float32)
    half = block.shape[-1] // 2
    turned = pltpu.roll(block, half, 2)
    low = lax.broadcasted_iota(jnp.int32, block.shape, 2) < half
    return jnp.where(low, -turned, turned).astype(jnp.bfloat16)


def local(eigvecs, gauge_links, perambulators, momenta):
    spaces = lax.axis_size("space")
    z_total = spaces // YB
    nev, sites = eigvecs.shape[3], eigvecs.shape[5]
    block_index = lax.axis_index("space")
    y_block = block_index % YB
    z_index = block_index // YB
    op_count = momenta.shape[0]
    v = eigvecs.reshape(6, nev, sites)
    u = gauge_links.reshape(3, 18, sites)

    def along(value, z_steps, y_steps):
        pairs = []
        for s in range(spaces):
            z, y = s // YB, s % YB
            pairs.append((s, (z + z_steps) % z_total * YB + (y + y_steps) % YB))
        return lax.ppermute(value, "space", pairs)

    cos_all, sin_all = phases(momenta, z_index, y_block * (sites // LX), sites, z_total)
    t_all = perambulators.shape[1]
    pair_count = perambulators.shape[3] * perambulators.shape[4]
    blocks = perambulators.reshape(t_all, 2, pair_count * nev, nev)
    both = jnp.concatenate([blocks[:, 0], blocks[:, 1]], axis=2)

    lanes = -(-sites // 128) * 128
    norm_scale = 1.0 / math.sqrt(3.0 * z_total * LX * LX)
    slices = lax.axis_size("tm")
    if (
        z_total == 2
        and lanes >= 6 * LX
        and op_count % (2 * spaces) == 0
        and t_all == slices
        and pair_count % 2 == 0
        and spaces <= 2 * slices
    ):
        ops, width = op_count // spaces, 2 * nev
        peers = max(spaces, slices)
        smeared, every, gathered = pl.pallas_call(
            functools.partial(whole_kernel, spaces, slices, norm_scale),
            out_shape=(
                jax.ShapeDtypeStruct((6, nev, sites), jnp.bfloat16),
                jax.ShapeDtypeStruct((op_count, nev, width), jnp.bfloat16),
                jax.ShapeDtypeStruct((spaces, 2 * ops, width), jnp.float32),
            ),
            in_specs=[pl.BlockSpec(memory_space=pltpu.VMEM)] * 5,
            out_specs=[pl.BlockSpec(memory_space=pltpu.VMEM)] * 3,
            scratch_shapes=[
                pltpu.VMEM((6, nev, lanes), jnp.float32),
                pltpu.VMEM((6, nev, sites), jnp.float32),
                pltpu.VMEM((6, nev, lanes), jnp.float32),
                pltpu.VMEM((6, nev, sites), jnp.float32),
                pltpu.VMEM((6, nev, sites), jnp.bfloat16),
                pltpu.VMEM((6, nev, sites), jnp.bfloat16),
                pltpu.VMEM((18, sites), jnp.float32),
                pltpu.VMEM((2, nev, lanes), jnp.float32),
                pltpu.VMEM((2, nev, lanes), jnp.float32),
                pltpu.SemaphoreType.DMA((4,)),
                pltpu.SemaphoreType.DMA((4,)),
                pltpu.VMEM((op_count, nev, width), jnp.float32),
                pltpu.VMEM((spaces, ops, nev, width), jnp.float32),
                pltpu.VMEM((spaces // 2, ops, nev, width), jnp.float32),
                pltpu.VMEM((slices, ops, nev, width), jnp.bfloat16),
                pltpu.VMEM((pair_count * nev, ops * width), jnp.bfloat16),
                pltpu.VMEM((t_all, pair_count * nev, width), jnp.bfloat16),
                pltpu.VMEM((ops * width, width), jnp.bfloat16),
                pltpu.VMEM((2 * ops, width), jnp.float32),
                pltpu.SemaphoreType.DMA((6, peers)),
                pltpu.SemaphoreType.DMA((6, peers)),
            ],
            compiler_params=pltpu.CompilerParams(
                collective_id=0, has_side_effects=True, vmem_limit_bytes=VMEM_LIMIT
            ),
            name="whole",
        )(v, u, cos_all, sin_all, both)
        found = gathered[:, :, :t_all].reshape(spaces, 2, ops, t_all)
        correlator = jnp.swapaxes(found, 0, 1).reshape(2, op_count, 1, t_all)
        elementals = jnp.swapaxes(every.reshape(op_count, nev, 2, nev), 1, 2)[:, None]
        return (smeared.reshape(eigvecs.shape), elementals, correlator)

    narrow = v.astype(jnp.bfloat16)
    up = along(narrow, -1, 0)
    down = up if z_total == 2 else along(narrow, 1, 0)
    zlink = along(u[2], 1, 0)
    edge = jnp.stack(
        link_times(
            lambda k: u[1, k : k + 1, sites - LX :], lambda i: v[i, :, sites - LX :], True
        )
    )
    row_above = along(v[:, :, :LX], 0, -1)
    row_below = along(edge, 0, 1)
    smeared, partial_sums = pl.pallas_call(
        functools.partial(smear_kernel, 1.0 / math.sqrt(3.0 * z_total * LX * LX)),
        out_shape=(
            jax.ShapeDtypeStruct((6, nev, sites), jnp.bfloat16),
            jax.ShapeDtypeStruct((op_count, nev, 2 * nev), jnp.float32),
        ),
        scratch_shapes=[
            pltpu.VMEM((6, nev, lanes), jnp.float32),
            pltpu.VMEM((6, nev, sites), jnp.float32),
            pltpu.VMEM((6, nev, lanes), jnp.float32),
            pltpu.VMEM((6, nev, sites), jnp.float32),
        ],
        compiler_params=pltpu.CompilerParams(vmem_limit_bytes=VMEM_LIMIT),
        name="smear",
    )(v, up, down, u, zlink, row_above, row_below, cos_all, sin_all)

    if op_count % spaces == 0:
        own = lax.psum_scatter(partial_sums, "space", scatter_dimension=0, tiled=True)
        own = own.astype(jnp.bfloat16)
        every = lax.all_gather(own, "space", axis=0, tiled=True)
    else:
        every = lax.psum(partial_sums, "space").astype(jnp.bfloat16)
        slots = -(-op_count // spaces)
        ids = jnp.minimum(block_index * slots + jnp.arange(slots), op_count - 1)
        own = jnp.take(every, ids, axis=0)
    ops = own.shape[0]
    far = lax.all_gather(own, "tm", axis=0)
    wide = own.astype(jnp.float32)
    near_re = jnp.swapaxes(wide[:, :, :nev], 1, 2)
    near_im = jnp.swapaxes(wide[:, :, nev:], 1, 2)
    g_re = jnp.concatenate([near_re, -near_im], axis=2)
    g_im = jnp.concatenate([near_im, near_re], axis=2)
    width = 2 * nev
    traces = pl.pallas_call(
        trace_kernel,
        grid=(t_all,),
        out_shape=jax.ShapeDtypeStruct((t_all, 2 * ops, width), jnp.float32),
        in_specs=[
            pl.BlockSpec((1, ops, nev, width), lambda t: (t, 0, 0, 0)),
            pl.BlockSpec((1, pair_count * nev, width), lambda t: (t, 0, 0)),
            pl.BlockSpec((ops, nev, width), lambda t: (0, 0, 0)),
            pl.BlockSpec((ops, nev, width), lambda t: (0, 0, 0)),
        ],
        out_specs=pl.BlockSpec((1, 2 * ops, width), lambda t: (t, 0, 0)),
        scratch_shapes=[
            pltpu.VMEM((pair_count * nev, ops * width), jnp.bfloat16),
            pltpu.VMEM((pair_count * nev, width), jnp.bfloat16),
            pltpu.VMEM((ops * width, width), jnp.bfloat16),
        ],
        compiler_params=pltpu.CompilerParams(vmem_limit_bytes=VMEM_LIMIT),
        name="traces",
    )(far, both, g_re, g_im)
    terms = lax.all_gather(traces[:, :, 0].reshape(t_all, 2, ops), "space", axis=0)
    terms = jnp.transpose(terms, (2, 0, 3, 1)).reshape(2, spaces * ops, t_all)
    correlator = terms[:, :op_count, None, :]
    elementals = jnp.swapaxes(every.reshape(op_count, nev, 2, nev), 1, 2)[:, None]
    return (smeared.reshape(eigvecs.shape), elementals, correlator)


def solution(mesh):
    return jax.shard_map(
        local,
        mesh=mesh,
        in_specs=(
            P("tm", None, None, None, "space", None),
            P(None, "tm", None, None, None, "space", None),
            P("tm", None, None, None, None, None, None),
            P(),
        ),
        out_specs=(
            P("tm", None, None, None, "space", None),
            P(None, "tm", None, None, None),
            P(None, None, "tm", None),
        ),
        check_vma=False,
    )
```

```python
import functools
import math

import jax
import jax.numpy as jnp
from jax import lax
from jax.experimental import pallas as pl
from jax.experimental.pallas import tpu as pltpu
from jax.sharding import PartitionSpec as P

LX = 24
YB = 4
KAPPA = 0.25
VMEM_LIMIT = 40 * 1024 * 1024
NT_DIMS = (((1,), (1,)), ((), ()))


def phases(momenta, z_index, y_start, site_count, z_total):
    site_index = jnp.arange(site_count, dtype=jnp.int32)
    x_coord = site_index % LX
    y_coord = y_start + site_index // LX
    turn_x = momenta[:, 0, None] * x_coord[None] % LX
    turn_y = momenta[:, 1, None] * y_coord[None] % LX
    turn_z = momenta[:, 2, None] * z_index % z_total
    angles = (
        2.0
        * math.pi
        * (
            turn_x.astype(jnp.float32) / LX
            + turn_y.astype(jnp.float32) / LX
            + turn_z.astype(jnp.float32) / z_total
        )
    )
    return jnp.cos(angles), -jnp.sin(angles)


def link_times(link, vector, adjoint):
    real, imag = [], []
    for row in range(3):
        out_re = out_im = None
        for colour in range(3):
            k = colour * 3 + row if adjoint else row * 3 + colour
            a, b = link(k), link(9 + k)
            if adjoint:
                b = -b
            x, y = vector(colour), vector(3 + colour)
            term_re = a * x - b * y
            term_im = a * y + b * x
            out_re = term_re if out_re is None else out_re + term_re
            out_im = term_im if out_im is None else out_im + term_im
        real.append(out_re)
        imag.append(out_im)
    return real + imag


def signed_roll(block, sign_low):
    half = block.shape[-1] // 2
    lane = lax.broadcasted_iota(jnp.int32, block.shape, 1)
    turned = pltpu.roll(block, half, 1)
    low = lane < half
    return jnp.where(low, sign_low * turned, -sign_low * turned)


def smear_kernel(
    norm_scale, v, up, down, u, zb, ra, rb, cs, sn, sm, elem, pad, wide, rows, sums
):
    nev, sites = v.shape[1], v.shape[2]
    lanes = pad.shape[2]
    lane = lax.broadcasted_iota(jnp.int32, (nev, lanes), 1)
    x_coord = lane % LX
    for i in range(6):
        pad[i, :, :sites] = v[i]
        sums[i] = (1.0 - 6.0 * KAPPA) * v[i]

    def add(terms):
        for i in range(6):
            sums[i] = sums[i] + KAPPA * terms[i]

    def link(d):
        return lambda k: u[d, k : k + 1, :]

    def forward_x(i):
        full = pad[i]
        return jnp.where(
            x_coord == LX - 1, pltpu.roll(full, LX - 1, 1), pltpu.roll(full, lanes - 1, 1)
        )[:, :sites]

    def forward_y(i):
        full = pad[i]
        return jnp.where(
            lane >= sites - LX,
            pltpu.roll(rows[i], sites - LX, 1),
            pltpu.roll(full, lanes - LX, 1),
        )[:, :sites]

    for i in range(6):
        rows[i, :, :LX] = ra[i].astype(jnp.float32)
    add(link_times(link(0), forward_x, False))
    add(link_times(link(1), forward_y, False))
    add(link_times(link(2), lambda i: up[i].astype(jnp.float32), False))
    add(link_times(lambda k: zb[k : k + 1, :], lambda i: down[i].astype(jnp.float32), True))
    for i, term in enumerate(link_times(link(0), lambda i: v[i], True)):
        pad[i, :, :sites] = term
    add(
        [
            jnp.where(
                x_coord == 0, pltpu.roll(pad[i], lanes - LX + 1, 1), pltpu.roll(pad[i], 1, 1)
            )[:, :sites]
            for i in range(6)
        ]
    )
    for i, term in enumerate(link_times(link(1), lambda i: v[i], True)):
        pad[i, :, :sites] = term
    for i in range(6):
        rows[i, :, :LX] = rb[i].astype(jnp.float32)
    add(
        [
            jnp.where(lane < LX, rows[i], pltpu.roll(pad[i], LX, 1))[:, :sites]
            for i in range(6)
        ]
    )
    for i in range(6):
        rounded = sums[i].astype(jnp.bfloat16)
        sm[i] = rounded
        wide[i] = rounded.astype(jnp.float32)

    form_elementals(norm_scale, cs, sn, sm, wide, elem, 0, elem.shape[0])


def form_elementals(norm_scale, cs, sn, sm, wide, elem, first, count):
    nev = wide.shape[1]
    per = 2 if count % 2 == 0 else 1

    def step(k, carry):
        start = first + k * per
        product = None
        for colour in range(3):
            s_re, s_im = wide[colour], wide[3 + colour]
            parts = []
            for j in range(per):
                cos_row = cs[pl.ds(start + j, 1), :]
                sin_row = sn[pl.ds(start + j, 1), :]
                parts.append((s_re * cos_row - s_im * sin_row).astype(jnp.bfloat16))
                parts.append((s_re * sin_row + s_im * cos_row).astype(jnp.bfloat16))
            left = jnp.concatenate([sm[colour], sm[3 + colour]], axis=0)
            term = lax.dot_general(
                left, jnp.concatenate(parts, axis=0), NT_DIMS, preferred_element_type=jnp.float32
            )
            product = term if product is None else product + term
        for j in range(per):
            block = product[:, j * 2 * nev : (j + 1) * 2 * nev]
            elem[start + j] = norm_scale * (block[:nev] + signed_roll(block[nev:], 1.0))
        return carry

    lax.fori_loop(0, count // per, step, 0)


def whole_kernel(
    spaces,
    slices,
    norm_scale,
    v,
    u,
    cs,
    sn,
    bc,
    sm,
    every,
    gathered,
    pad,
    wide,
    prod,
    sums,
    narrow,
    other,
    zb,
    edge,
    got,
    send,
    recv,
    elem,
    *rest,
):
    me, mine = lax.axis_index("space"), lax.axis_index("tm")
    nev, sites = v.shape[1], v.shape[2]
    lanes = pad.shape[2]
    z, y = me // YB, me % YB
    across = (me + YB) % spaces
    above = z * YB + (y + 1) % YB
    below = z * YB + (y + YB - 1) % YB
    barrier = pltpu.get_barrier_semaphore()
    for d in range(1, spaces):
        pl.semaphore_signal(
            barrier, inc=1, device_id=((me + d) % spaces, mine), device_id_type=pl.DeviceIdType.MESH
        )
    for d in range(1, slices):
        pl.semaphore_signal(
            barrier, inc=1, device_id=(me, (mine + d) % slices), device_id_type=pl.DeviceIdType.MESH
        )

    def remote(k, source, target, device):
        return pltpu.make_async_remote_copy(
            src_ref=source,
            dst_ref=target,
            send_sem=send.at[k],
            recv_sem=recv.at[k],
            device_id=(device, mine),
            device_id_type=pl.DeviceIdType.MESH,
        )

    for i in range(6):
        narrow[i] = v[i].astype(jnp.bfloat16)
    pl.semaphore_wait(barrier, spaces + slices - 2)
    copies = [
        remote(0, narrow, other, across),
        remote(1, u.at[2], zb, across),
        remote(2, edge.at[0], got.at[0], below),
        remote(3, edge.at[1], got.at[1], above),
    ]
    copies[0].start()
    copies[1].start()
    lane = lax.broadcasted_iota(jnp.int32, (nev, lanes), 1)
    x_coord = lane % LX
    last = sites - LX
    pad[...] = jnp.zeros_like(pad)
    prod[...] = jnp.zeros_like(prod)
    for i in range(6):
        pad[i, :, :sites] = v[i]
        sums[i] = (1.0 - 6.0 * KAPPA) * v[i]

    def add(terms):
        for i in range(6):
            sums[i] = sums[i] + KAPPA * terms[i]

    def link(d):
        return lambda k: u[d, k : k + 1, :]

    for i, term in enumerate(link_times(link(1), lambda i: v[i], True)):
        prod[i, :, :sites] = term
    for side, (ref, start) in enumerate(((pad, 0), (prod, last))):
        packed = jnp.zeros((nev, lanes), jnp.float32)
        for i in range(6):
            inside = jnp.logical_and(lane >= i * LX, lane < (i + 1) * LX)
            packed = jnp.where(
                inside, pltpu.roll(ref[i], (i * LX - start + lanes) % lanes, 1), packed
            )
        edge[side] = packed
    copies[2].start()
    copies[3].start()

    def forward_x(i):
        return jnp.where(
            x_coord == LX - 1, pltpu.roll(pad[i], LX - 1, 1), pltpu.roll(pad[i], lanes - 1, 1)
        )[:, :sites]

    def forward_y(i):
        return jnp.where(
            lane >= last,
            pltpu.roll(got[0], (last - i * LX + lanes) % lanes, 1),
            pltpu.roll(pad[i], lanes - LX, 1),
        )[:, :sites]

    def behind_y(i):
        return jnp.where(
            lane < LX,
            pltpu.roll(got[1], (lanes - i * LX) % lanes, 1),
            pltpu.roll(prod[i], LX, 1),
        )[:, :sites]

    add(link_times(link(0), forward_x, False))
    for i, term in enumerate(link_times(link(0), lambda i: v[i], True)):
        wide[i] = term
    copies[2].wait_recv()
    copies[3].wait_recv()
    add(link_times(link(1), forward_y, False))
    add([behind_y(i) for i in range(6)])
    for i in range(6):
        prod[i, :, :sites] = wide[i]
    add(
        [
            jnp.where(
                x_coord == 0, pltpu.roll(prod[i], lanes - LX + 1, 1), pltpu.roll(prod[i], 1, 1)
            )[:, :sites]
            for i in range(6)
        ]
    )
    copies[0].wait_recv()
    copies[1].wait_recv()
    add(link_times(link(2), lambda i: other[i].astype(jnp.float32), False))
    add(link_times(lambda k: zb[k : k + 1, :], lambda i: other[i].astype(jnp.float32), True))
    for i in range(6):
        rounded = sums[i].astype(jnp.bfloat16)
        sm[i] = rounded
        wide[i] = rounded.astype(jnp.float32)

    ops = elem.shape[0] // spaces

    def form(device):
        form_elementals(norm_scale, cs, sn, sm, wide, elem, device * ops, ops)

    exchange(form, spaces, slices, elem, bc, every, gathered, *rest)
    for copy in copies:
        copy.wait_send()


def trace_kernel(far, bc, g_re, g_im, out, left, b2, weights):
    ops = far.shape[1]
    nev, width = far.shape[2], far.shape[3]
    pairs = bc.shape[1] // nev
    for p in range(ops):
        block = far[0, p].astype(jnp.float32)
        weights[2 * p * nev : (2 * p + 1) * nev, :] = far[0, p]
        weights[(2 * p + 1) * nev : (2 * p + 2) * nev, :] = signed_roll(block, -1.0).astype(
            jnp.bfloat16
        )
    left[...] = lax.dot_general(
        bc[0], weights[...], NT_DIMS, preferred_element_type=jnp.float32
    ).astype(jnp.bfloat16)
    b2[...] = signed_roll(bc[0].astype(jnp.float32), -1.0).astype(jnp.bfloat16)
    right = None
    for q in range(0, pairs, 2):
        spans = [slice(k * nev, (k + 1) * nev) for k in (q, q + 1)]
        stacked = jnp.concatenate(
            [
                jnp.concatenate([left[s, p * width : (p + 1) * width] for s in spans], axis=1)
                for p in range(ops)
            ],
            axis=0,
        )
        facing = jnp.concatenate(
            [
                jnp.concatenate([bc[0, s, :] for s in spans], axis=1),
                jnp.concatenate([b2[s, :] for s in spans], axis=1),
            ],
            axis=0,
        )
        term = lax.dot_general(stacked, facing, NT_DIMS, preferred_element_type=jnp.float32)
        right = term if right is None else right + term
    for part, g in enumerate((g_re, g_im)):
        for p in range(ops):
            total = jnp.sum(g[p] * right[p * nev : (p + 1) * nev], keepdims=True) / nev
            out[0, part * ops + p : part * ops + p + 1, :] = jnp.broadcast_to(total, (1, width))


def exchange(
    form, spaces, slices, partial, blocks, every, gathered, inbox, middle, far, left, bc, b2, weights, tile, send, recv
):
    me, mine = lax.axis_index("space"), lax.axis_index("tm")
    ops, nev, width = inbox.shape[1:]
    pairs = bc.shape[1] // nev

    depth, side, level = spaces // 2, me % 2, me // 2
    partner = me + 1 - 2 * side

    def remote(kind, d, source, target, device):
        return pltpu.make_async_remote_copy(
            src_ref=source,
            dst_ref=target,
            send_sem=send.at[kind, d],
            recv_sem=recv.at[kind, d],
            device_id=device,
            device_id_type=pl.DeviceIdType.MESH,
        )

    def block_of(ref, device):
        return ref.at[pl.ds(device * ops, ops)]

    order = list(range(depth - 1, -1, -1))
    beside, along = {}, {}

    def hand_on(d):
        beside[d].wait_recv()
        there = (level + d) % depth * 2
        total = partial[pl.ds((there + side) * ops, ops)] + inbox[d]
        if d > 0:
            middle[d] = total
            along[d] = remote(1, d, middle.at[d], inbox.at[depth + d], (there + side, mine))
            along[d].start()
        return total

    for k, d in enumerate(order):
        there = (level + d) % depth * 2
        form(there + 1 - side)
        beside[d] = remote(
            0, d, block_of(partial, there + 1 - side), inbox.at[d], (partner, mine)
        )
        beside[d].start()
        form(there + side)
        if k > 0:
            hand_on(order[k - 1])
    for t in range(blocks.shape[0]):
        re, im = blocks[t, 0], blocks[t, 1]
        bc[t] = jnp.concatenate([re, im], axis=1)
        b2[t] = jnp.concatenate([-im, re], axis=1)
    total = hand_on(0)
    for d in order[:-1]:
        along[d].wait_recv()
        total = total + inbox[depth + d]
    rounded = total.astype(jnp.bfloat16)
    far[mine] = rounded
    every[pl.ds(me * ops, ops)] = rounded

    def far_copy(d):
        return remote(3, d, far.at[mine], far.at[mine], (me, (mine + d) % slices))

    def share_copy(d):
        there = (level + d) % depth * 2 + side
        return remote(4, d, far.at[mine], block_of(every, me), (there, mine))

    def pass_copy(d):
        origin = (level + depth - d) % depth * 2 + side
        return remote(5, d, block_of(every, origin), block_of(every, origin), (partner, mine))

    for d in range(1, slices):
        far_copy(d).start()
    for d in range(1, depth):
        share_copy(d).start()
    own_pass = remote(5, 0, far.at[mine], block_of(every, me), (partner, mine))
    own_pass.start()

    near = rounded.astype(jnp.float32)
    low = lax.broadcasted_iota(jnp.int32, (nev, width), 1) < nev
    near_re, near_im = [], []
    for p in range(0, ops, 2):
        one, two = near[p], near[p + 1]
        near_re.append(jnp.where(low, one, pltpu.roll(two, nev, 1)))
        near_im.append(jnp.where(low, pltpu.roll(one, nev, 1), two))
    near_re = jnp.concatenate(near_re, axis=1)
    near_im = jnp.concatenate(near_im, axis=1)
    row_id = lax.broadcasted_iota(jnp.int32, (2 * ops, width), 0)
    lane_id = lax.broadcasted_iota(jnp.int32, (2 * ops, width), 1)
    low_row = lax.broadcasted_iota(jnp.int32, (1, width), 1) < nev
    tile[...] = jnp.zeros_like(tile)

    def step(d, carry):
        @pl.when(d > 0)
        def _():
            far_copy(d).wait_recv()

        @pl.when(jnp.logical_and(d > 0, d < depth))
        def _():
            share_copy(d).wait_recv()
            pass_copy(d).start()

        t0 = (mine + slices - d) % slices
        for p in range(ops):
            block = far[t0, p]
            weights[2 * p * nev : (2 * p + 1) * nev, :] = block
            weights[(2 * p + 1) * nev : (2 * p + 2) * nev, :] = signed_roll(
                block.astype(jnp.float32), -1.0
            ).astype(jnp.bfloat16)
        left[...] = lax.dot_general(
            bc[t0], weights[...], NT_DIMS, preferred_element_type=jnp.float32
        ).astype(jnp.bfloat16)
        right = None
        for q in range(0, pairs, 2):
            spans = [slice(k * nev, (k + 1) * nev) for k in (q, q + 1)]
            stacked = jnp.concatenate(
                [
                    jnp.concatenate([left[s, p * width : (p + 1) * width] for s in spans], axis=1)
                    for p in range(ops)
                ],
                axis=0,
            )
            facing = jnp.concatenate(
                [
                    jnp.concatenate([bc[t0, s, :] for s in spans], axis=1),
                    jnp.concatenate([b2[t0, s, :] for s in spans], axis=1),
                ],
                axis=0,
            )
            term = lax.dot_general(facing, stacked, NT_DIMS, preferred_element_type=jnp.float32)
            right = term if right is None else right + term
        r_re, r_im = right[:nev], right[nev:]
        rows = (
            jnp.sum(near_re * r_re - near_im * r_im, axis=0, keepdims=True),
            jnp.sum(near_re * r_im + near_im * r_re, axis=0, keepdims=True),
        )
        found = tile[...]
        for part in range(2):
            for p in range(ops):
                half = rows[part][:, p // 2 * width : (p // 2 + 1) * width]
                keep = low_row if p % 2 == 0 else jnp.logical_not(low_row)
                value = jnp.sum(jnp.where(keep, half, 0.0), axis=1, keepdims=True) / nev
                spot = jnp.logical_and(row_id == part * ops + p, lane_id == t0)
                found = jnp.where(spot, value, found)
        tile[...] = found
        return carry

    lax.fori_loop(0, slices, step, 0)
    gathered[me] = tile[...]
    ends = [
        remote(2, d, tile, gathered.at[me], ((me + d) % spaces, mine)) for d in range(1, spaces)
    ]
    for copy in ends:
        copy.start()
    passes = [own_pass] + [pass_copy(d) for d in range(1, depth)]
    for copy in passes + ends:
        copy.wait_recv()
    shares = [share_copy(d) for d in range(1, depth)]
    fars = [far_copy(d) for d in range(1, slices)]
    for copy in list(beside.values()) + list(along.values()) + fars + shares + passes + ends:
        copy.wait_send()


def local(eigvecs, gauge_links, perambulators, momenta):
    spaces = lax.axis_size("space")
    z_total = spaces // YB
    nev, sites = eigvecs.shape[3], eigvecs.shape[5]
    block_index = lax.axis_index("space")
    y_block = block_index % YB
    z_index = block_index // YB
    op_count = momenta.shape[0]
    v = eigvecs.reshape(6, nev, sites)
    u = gauge_links.reshape(3, 18, sites)

    def along(value, z_steps, y_steps):
        pairs = []
        for s in range(spaces):
            z, y = s // YB, s % YB
            pairs.append((s, (z + z_steps) % z_total * YB + (y + y_steps) % YB))
        return lax.ppermute(value, "space", pairs)

    cos_all, sin_all = phases(momenta, z_index, y_block * (sites // LX), sites, z_total)
    t_all = perambulators.shape[1]
    pair_count = perambulators.shape[3] * perambulators.shape[4]
    blocks = perambulators.reshape(t_all, 2, pair_count * nev, nev)
    both = jnp.concatenate([blocks[:, 0], blocks[:, 1]], axis=2)

    lanes = -(-sites // 128) * 128
    norm_scale = 1.0 / math.sqrt(3.0 * z_total * LX * LX)
    slices = lax.axis_size("tm")
    if (
        z_total == 2
        and lanes >= 6 * LX
        and op_count % (2 * spaces) == 0
        and t_all == slices
        and pair_count % 2 == 0
        and spaces <= 2 * slices
    ):
        ops, width = op_count // spaces, 2 * nev
        peers = max(spaces, slices)
        smeared, every, gathered = pl.pallas_call(
            functools.partial(whole_kernel, spaces, slices, norm_scale),
            out_shape=(
                jax.ShapeDtypeStruct((6, nev, sites), jnp.bfloat16),
                jax.ShapeDtypeStruct((op_count, nev, width), jnp.bfloat16),
                jax.ShapeDtypeStruct((spaces, 2 * ops, width), jnp.float32),
            ),
            in_specs=[pl.BlockSpec(memory_space=pltpu.VMEM)] * 5,
            out_specs=[pl.BlockSpec(memory_space=pltpu.VMEM)] * 3,
            scratch_shapes=[
                pltpu.VMEM((6, nev, lanes), jnp.float32),
                pltpu.VMEM((6, nev, sites), jnp.float32),
                pltpu.VMEM((6, nev, lanes), jnp.float32),
                pltpu.VMEM((6, nev, sites), jnp.float32),
                pltpu.VMEM((6, nev, sites), jnp.bfloat16),
                pltpu.VMEM((6, nev, sites), jnp.bfloat16),
                pltpu.VMEM((18, sites), jnp.float32),
                pltpu.VMEM((2, nev, lanes), jnp.float32),
                pltpu.VMEM((2, nev, lanes), jnp.float32),
                pltpu.SemaphoreType.DMA((4,)),
                pltpu.SemaphoreType.DMA((4,)),
                pltpu.VMEM((op_count, nev, width), jnp.float32),
                pltpu.VMEM((spaces, ops, nev, width), jnp.float32),
                pltpu.VMEM((spaces // 2, ops, nev, width), jnp.float32),
                pltpu.VMEM((slices, ops, nev, width), jnp.bfloat16),
                pltpu.VMEM((pair_count * nev, ops * width), jnp.bfloat16),
                pltpu.VMEM((t_all, pair_count * nev, width), jnp.bfloat16),
                pltpu.VMEM((t_all, pair_count * nev, width), jnp.bfloat16),
                pltpu.VMEM((ops * width, width), jnp.bfloat16),
                pltpu.VMEM((2 * ops, width), jnp.float32),
                pltpu.SemaphoreType.DMA((6, peers)),
                pltpu.SemaphoreType.DMA((6, peers)),
            ],
            compiler_params=pltpu.CompilerParams(
                collective_id=0, has_side_effects=True, vmem_limit_bytes=VMEM_LIMIT
            ),
            name="whole",
        )(v, u, cos_all, sin_all, blocks)
        found = gathered[:, :, :t_all].reshape(spaces, 2, ops, t_all)
        correlator = jnp.swapaxes(found, 0, 1).reshape(2, op_count, 1, t_all)
        elementals = jnp.swapaxes(every.reshape(op_count, nev, 2, nev), 1, 2)[:, None]
        return (smeared.reshape(eigvecs.shape), elementals, correlator)

    narrow = v.astype(jnp.bfloat16)
    up = along(narrow, -1, 0)
    down = up if z_total == 2 else along(narrow, 1, 0)
    zlink = along(u[2], 1, 0)
    edge = jnp.stack(
        link_times(
            lambda k: u[1, k : k + 1, sites - LX :], lambda i: v[i, :, sites - LX :], True
        )
    )
    row_above = along(v[:, :, :LX], 0, -1)
    row_below = along(edge, 0, 1)
    smeared, partial_sums = pl.pallas_call(
        functools.partial(smear_kernel, 1.0 / math.sqrt(3.0 * z_total * LX * LX)),
        out_shape=(
            jax.ShapeDtypeStruct((6, nev, sites), jnp.bfloat16),
            jax.ShapeDtypeStruct((op_count, nev, 2 * nev), jnp.float32),
        ),
        scratch_shapes=[
            pltpu.VMEM((6, nev, lanes), jnp.float32),
            pltpu.VMEM((6, nev, sites), jnp.float32),
            pltpu.VMEM((6, nev, lanes), jnp.float32),
            pltpu.VMEM((6, nev, sites), jnp.float32),
        ],
        compiler_params=pltpu.CompilerParams(vmem_limit_bytes=VMEM_LIMIT),
        name="smear",
    )(v, up, down, u, zlink, row_above, row_below, cos_all, sin_all)

    if op_count % spaces == 0:
        own = lax.psum_scatter(partial_sums, "space", scatter_dimension=0, tiled=True)
        own = own.astype(jnp.bfloat16)
        every = lax.all_gather(own, "space", axis=0, tiled=True)
    else:
        every = lax.psum(partial_sums, "space").astype(jnp.bfloat16)
        slots = -(-op_count // spaces)
        ids = jnp.minimum(block_index * slots + jnp.arange(slots), op_count - 1)
        own = jnp.take(every, ids, axis=0)
    ops = own.shape[0]
    far = lax.all_gather(own, "tm", axis=0)
    wide = own.astype(jnp.float32)
    near_re = jnp.swapaxes(wide[:, :, :nev], 1, 2)
    near_im = jnp.swapaxes(wide[:, :, nev:], 1, 2)
    g_re = jnp.concatenate([near_re, -near_im], axis=2)
    g_im = jnp.concatenate([near_im, near_re], axis=2)
    width = 2 * nev
    traces = pl.pallas_call(
        trace_kernel,
        grid=(t_all,),
        out_shape=jax.ShapeDtypeStruct((t_all, 2 * ops, width), jnp.float32),
        in_specs=[
            pl.BlockSpec((1, ops, nev, width), lambda t: (t, 0, 0, 0)),
            pl.BlockSpec((1, pair_count * nev, width), lambda t: (t, 0, 0)),
            pl.BlockSpec((ops, nev, width), lambda t: (0, 0, 0)),
            pl.BlockSpec((ops, nev, width), lambda t: (0, 0, 0)),
        ],
        out_specs=pl.BlockSpec((1, 2 * ops, width), lambda t: (t, 0, 0)),
        scratch_shapes=[
            pltpu.VMEM((pair_count * nev, ops * width), jnp.bfloat16),
            pltpu.VMEM((pair_count * nev, width), jnp.bfloat16),
            pltpu.VMEM((ops * width, width), jnp.bfloat16),
        ],
        compiler_params=pltpu.CompilerParams(vmem_limit_bytes=VMEM_LIMIT),
        name="traces",
    )(far, both, g_re, g_im)
    terms = lax.all_gather(traces[:, :, 0].reshape(t_all, 2, ops), "space", axis=0)
    terms = jnp.transpose(terms, (2, 0, 3, 1)).reshape(2, spaces * ops, t_all)
    correlator = terms[:, :op_count, None, :]
    elementals = jnp.swapaxes(every.reshape(op_count, nev, 2, nev), 1, 2)[:, None]
    return (smeared.reshape(eigvecs.shape), elementals, correlator)


def solution(mesh):
    return jax.shard_map(
        local,
        mesh=mesh,
        in_specs=(
            P("tm", None, None, None, "space", None),
            P(None, "tm", None, None, None, "space", None),
            P("tm", None, None, None, None, None, None),
            P(),
        ),
        out_specs=(
            P("tm", None, None, None, "space", None),
            P(None, "tm", None, None, None),
            P(None, None, "tm", None),
        ),
        check_vma=False,
    )
```
